256 devices in a mesh: row: 8 (over y_hi, x), cent: 32 (over y_lo, z, core).
Axes of the slice: x: 4, y: 4 (y_hi: 2, y_lo: 2; y = y_hi * 2 + y_lo), z: 8, core: 2. Of those that a mesh axis runs over, the one named last changes fastest.
Arguments:
- embeddings: bfloat16 [65536, 1024], P('row', 'cent'), may hold values from -6 to 6
- assigned: int32 [65536], P('row'), may hold values from 0 to 8191
- centroids: bfloat16 [8192, 1024], P('cent'), may hold values from -0.1875 to 0.1875
Outputs:
- new_centroids: bfloat16 [8192, 1024], P('cent')
- best_cosine: float32 [65536], P('row')
The draws below stay inside these ranges and needn't reach their ends.
All inputs are finite; a program needn't handle non-finite values.
Results may differ from the reference program's by a relative error of at most 0.015.
Values may be sent and summed in bfloat16 or wider, within the bound.
A program may use at most 128 MiB of HBM per device.

```python
import jax
import jax.numpy as jnp
from jax import lax

D = 1024
ROW_DEV = 8192
K = 8192
N = 65536


def set_ends(drawn, rng, least, largest):
    spot = [jax.random.randint(jax.random.fold_in(rng, axis), (), 0, length) for axis, length in enumerate(drawn.shape)]
    main_axis = drawn.shape.index(max(drawn.shape))
    neighbour = spot[:main_axis] + [(spot[main_axis] + 1) % drawn.shape[main_axis]] + spot[main_axis + 1:]
    return drawn.at[tuple(spot)].set(least).at[tuple(neighbour)].set(largest)


def block_levels(rng, shape, pieces, smallest, high):
    def one(position, blocks):
        steps = jax.random.uniform(jax.random.fold_in(jax.random.fold_in(rng, 6), position), (blocks,), jnp.float32, smallest / len(pieces), high / len(pieces))
        return jnp.repeat(jnp.exp(steps), shape[position] // blocks).reshape((-1,) + (1,) * (len(shape) - position - 1))

    loudness = one(*pieces[0])
    for cut in pieces[1:]:
        loudness = loudness * one(*cut)
    return loudness


def centred(rng, dims, width, reach, cuts=(), dtype=jnp.bfloat16):
    array = width * jax.random.normal(rng, dims, jnp.float32)
    if cuts:
        array = array * block_levels(rng, dims, cuts, -0.22, 0.18)
    return jnp.clip(array, -reach, reach).astype(dtype)


def setup_inputs(seed: int = 0) -> dict:
    splits = jax.random.split(jax.random.key(seed), 4)
    embeddings = centred(splits[0], (N, D), 1.0, 6.0, ((0, 8), (1, 32)))
    assigned = set_ends(jax.random.randint(splits[1], (N,), 0, K), jax.random.fold_in(splits[1], 1), 0, K - 1).astype(jnp.int32)
    centroids = centred(splits[2], (K, D), D ** -0.5, 0.1875, ((0, 32),))
    return {"embeddings": embeddings, "assigned": assigned, "centroids": centroids}


def normalize_rows(values):
    return values * lax.rsqrt(lax.optimization_barrier(jnp.sum(values * values, axis=1, keepdims=True)) + 1e-06)

def reference(embeddings, assigned, centroids):
    wide = embeddings.astype(jnp.float32)
    unit = normalize_rows(wide).astype(jnp.bfloat16)
    blocks = N // ROW_DEV
    unit_blocks = unit.reshape(blocks, ROW_DEV, D)
    id_blocks = assigned.reshape(blocks, ROW_DEV)

    def add_block(total, pair):
        piece, ids = pair
        partial_sum = jax.ops.segment_sum(piece.astype(jnp.float32), ids, num_segments=K)
        rounded = lax.optimization_barrier(partial_sum.astype(jnp.bfloat16)).astype(jnp.float32)
        return (total + rounded, None)
    sums, _ = lax.scan(add_block, jnp.zeros((K, D), jnp.float32), (unit_blocks, id_blocks))
    new_centroids = normalize_rows(centroids.astype(jnp.float32) + sums).astype(jnp.bfloat16)
    wide_centroids = new_centroids.astype(jnp.float32)
    step_rows = min(512, N)

    def best_block(piece):
        scores = jnp.dot(piece.astype(jnp.float32), wide_centroids.T)
        return lax.optimization_barrier(jnp.max(scores, axis=1))
    best = lax.map(best_block, unit.reshape(N // step_rows, step_rows, D))
    return (new_centroids, best.reshape(N).astype(jnp.float32))
```

```python
import functools

import jax
import jax.numpy as jnp
from jax import lax
from jax.experimental import pallas as pl
from jax.experimental.pallas import tpu as pltpu
from jax.sharding import PartitionSpec as P

MESH = pl.DeviceIdType.MESH
F = 32
EPS = 1e-06


def kernel(nr, nz, x_ref, id_ref, cent_ref, nc_out, best_out,
           q, qr, myinv, inv, e, kr, acc, part, got, summed, turned, centbuf, ncs, top, tops,
           loc_sem, n_send, n_recv, i_send, i_recv, ez_send, ef_send, e_recv, c_send, c_recv,
           p_send, p_recv, s_send, s_recv, g_send, g_recv, t_send, t_recv):
    nc = 4 * nz
    rows = x_ref.shape[1]
    own_rows = rows // nc
    a_count = nz // 2
    tile_rows = rows // a_count
    j_count = 256 // nz
    r = lax.axis_index("row")
    c = lax.axis_index("cent")
    core = lax.rem(c, 2)
    z = lax.rem(c // 2, nz)
    y = c // (2 * nz)
    a = z // 2

    def cent_id(yy, zz, cc):
        return yy * (2 * nz) + zz * 2 + cc

    def remote(src, dst, send, recv, row, cent):
        return pltpu.make_async_remote_copy(
            src_ref=src, dst_ref=dst, send_sem=send, recv_sem=recv,
            device_id=(row, cent), device_id_type=MESH)

    def drain(ref, sem):
        pltpu.make_async_copy(ref, ref, sem).wait()

    def span(start, size):
        return pl.ds(pl.multiple_of(start, size), size)

    barrier = pltpu.get_barrier_semaphore()

    @pl.loop(1, nc)
    def _(i):
        pl.semaphore_signal(barrier, inc=1, device_id=(r, lax.rem(c + i, nc)), device_id_type=MESH)

    @pl.loop(1, nr)
    def _(i):
        pl.semaphore_signal(barrier, inc=1, device_id=(lax.rem(r + i, nr), c), device_id_type=MESH)

    step = min(1024, rows)

    @pl.loop(0, rows // step)
    def _(t):
        here = span(t * step, step)
        wide = x_ref[:, here].astype(jnp.float32)
        q[:, here] = jnp.sum(wide * wide, axis=0, keepdims=True)

    pl.semaphore_wait(barrier, nc - 1 + nr - 1)

    @pl.loop(1, nc)
    def _(i):
        d = lax.rem(c + i, nc)
        remote(q.at[:, span(d * own_rows, own_rows)], qr.at[c], n_send, n_recv, r, d).start()

    own = pltpu.make_async_copy(q.at[:, span(c * own_rows, own_rows)], qr.at[c], loc_sem.at[0])
    own.start()
    own_e = pltpu.make_async_copy(x_ref.at[:, span(a * tile_rows, tile_rows)], e.at[c], loc_sem.at[1])
    own_e.start()
    own_c = pltpu.make_async_copy(cent_ref.at[span(r * j_count, j_count), :], centbuf.at[a], loc_sem.at[2])
    own_c.start()
    own.wait()
    drain(qr.at[pl.ds(0, nc - 1)], n_recv)
    myinv[...] = lax.rsqrt(jnp.sum(qr[...], axis=0) + EPS)

    @pl.loop(1, nc)
    def _(i):
        d = lax.rem(c + i, nc)
        remote(myinv, inv.at[:, span(c * own_rows, own_rows)], i_send, i_recv, r, d).start()

    own_i = pltpu.make_async_copy(myinv, inv.at[:, span(c * own_rows, own_rows)], loc_sem.at[3])
    own_i.start()

    @pl.loop(1, nz)
    def _(i):
        zz = lax.rem(z + i, nz)
        d = cent_id(y, zz, core)
        remote(x_ref.at[:, span((zz // 2) * tile_rows, tile_rows)], e.at[c], ez_send, e_recv.at[c], r, d).start()

    @pl.loop(1, a_count)
    def _(i):
        d = cent_id(y, lax.rem(z + 2 * i, nz), core)
        remote(cent_ref.at[span(r * j_count, j_count), :], centbuf.at[a], c_send, c_recv, r, d).start()

    y_mate = cent_id(1 - y, z, core)
    core_mate = cent_id(y, z, 1 - core)

    def pass_on(piece, to_y):
        if to_y:
            remote(e.at[piece], e.at[piece], ef_send, e_recv.at[piece], r, y_mate).start()
        remote(e.at[piece], e.at[piece], ef_send, e_recv.at[piece], r, core_mate).start()

    def pass_z(i):
        half = (i + 1) // 2
        turn = half * (2 * lax.rem(i, 2) - 1) + nz
        piece = cent_id(y, lax.rem(z + turn, nz), core)
        drain(e.at[piece], e_recv.at[piece])
        pass_on(piece, True)

    def pass_y(i):
        piece = cent_id(1 - y, lax.rem(z + i, nz), core)
        drain(e.at[piece], e_recv.at[piece])
        pass_on(piece, False)

    own_e.wait()
    pass_on(c, True)

    own_i.wait()
    drain(inv.at[:, pl.ds(0, rows - own_rows)], i_recv)

    acc[...] = jnp.zeros_like(acc)
    klo_count = 4 * nr
    shift_c = nr * j_count

    @pl.loop(0, rows // step)
    def _(t):
        here = span(t * step, step)
        ids = id_ref[:, here]
        unit = (x_ref[:, here].astype(jnp.float32) * inv[:, here]).astype(jnp.bfloat16)
        cc = ids // shift_c
        rr = lax.rem(ids, shift_c) // j_count
        jj = lax.rem(ids, j_count)
        zz = lax.rem(cc // 2, nz)
        lane = lax.rem(cc, 2) * 128 + (zz // 2) * j_count + jj
        low = rr * 4 + (cc // (2 * nz)) * 2 + lax.rem(zz, 2)
        lane_b = jnp.broadcast_to(lane.astype(jnp.float32), (256, step)).astype(jnp.bfloat16)
        iota = lax.broadcasted_iota(jnp.int32, (256, step), 0).astype(jnp.float32).astype(jnp.bfloat16)
        one = jnp.bfloat16(1)
        nil = jnp.bfloat16(0)
        hot = jnp.where(lane_b == iota, one, nil)
        low_b = jnp.broadcast_to(low.astype(jnp.float32), (F, step)).astype(jnp.bfloat16)
        for j in range(klo_count):
            kr[j * F:(j + 1) * F, :] = jnp.where(low_b == jnp.bfloat16(j), unit, nil)
        acc[...] += lax.dot_general(kr[...], hot, (((1,), (1,)), ((), ())), preferred_element_type=jnp.float32)

    part[...] = acc[...].astype(jnp.bfloat16)

    @pl.loop(1, nr)
    def _(i):
        rr = lax.rem(r + i, nr)
        remote(part.at[span(rr * 128, 128), :], got.at[r], p_send, p_recv, rr, c).start()

    own_p = pltpu.make_async_copy(part.at[span(r * 128, 128), :], got.at[r], loc_sem.at[4])
    own_p.start()

    @pl.loop(1, nz // 2 + 1)
    def _(i):
        pass_z(i)

    own_p.wait()
    drain(got.at[pl.ds(0, nr - 1)], p_recv)
    total = got[0].astype(jnp.float32)
    for i in range(1, nr):
        total = total + got[i].astype(jnp.float32)
    summed[...] = total.astype(jnp.bfloat16)

    @pl.loop(1, nc)
    def _(i):
        d = lax.rem(c + i, nc)
        u = (d // (2 * nz)) * 2 + lax.rem(d // 2, 2)
        remote(summed.at[span(u * F, F), span(lax.rem(d, 2) * 128, 128)], turned.at[span(c * F, F), :],
               s_send, s_recv, r, d).start()

    u_own = y * 2 + lax.rem(z, 2)
    own_s = pltpu.make_async_copy(summed.at[span(u_own * F, F), span(core * 128, 128)],
                                  turned.at[span(c * F, F), :], loc_sem.at[5])
    own_s.start()
    own_c.wait()
    if a_count > 1:
        drain(centbuf.at[pl.ds(0, a_count - 1)], c_recv)
    old = centbuf[...].reshape(128, cent_ref.shape[1]).astype(jnp.float32)
    own_s.wait()
    drain(turned.at[pl.ds(0, (nc - 1) * F), :], s_recv)
    fresh = turned[...].astype(jnp.float32).T + old
    fresh = fresh * lax.rsqrt(jnp.sum(fresh * fresh, axis=1, keepdims=True) + EPS)
    ncs[r] = fresh.astype(jnp.bfloat16)

    @pl.loop(1, nr)
    def _(i):
        rr = lax.rem(r + i, nr)
        remote(ncs.at[r], ncs.at[r], g_send, g_recv, rr, c).start()

    @pl.loop(nz // 2 + 1, nz)
    def _(i):
        pass_z(i)

    @pl.loop(0, nz)
    def _(i):
        pass_y(i)

    @pl.loop(0, 2 * nz)
    def _(i):
        piece = cent_id(i // nz, lax.rem(i, nz), 1 - core)
        drain(e.at[piece], e_recv.at[piece])

    drain(ncs.at[pl.ds(0, nr - 1)], g_recv)
    for i in range(nr):
        nc_out[i * j_count:(i + 1) * j_count, :] = ncs[i, span(a * j_count, j_count), :]

    width = nc * F
    wide_rows = 256
    every = ncs[...].reshape(nr * 128, width)

    @pl.loop(0, tile_rows // wide_rows)
    def _(t):
        here = span(t * wide_rows, wide_rows)
        scores = jnp.dot(every, e[:, :, here].reshape(width, wide_rows), preferred_element_type=jnp.float32)
        top[:, here] = jnp.max(scores, axis=0, keepdims=True)

    @pl.loop(1, nc)
    def _(i):
        remote(top, tops.at[c], t_send, t_recv, r, lax.rem(c + i, nc)).start()

    own_t = pltpu.make_async_copy(top, tops.at[c], loc_sem.at[6])
    own_t.start()
    drain(qr.at[pl.ds(0, nc - 1)], n_send)
    drain(inv.at[:, pl.ds(0, rows - own_rows)], i_send)
    drain(e.at[pl.ds(0, nz - 1)], ez_send)
    drain(e.at[pl.ds(0, 3 * nz)], ef_send)
    if a_count > 1:
        drain(centbuf.at[pl.ds(0, a_count - 1)], c_send)
    drain(got.at[pl.ds(0, nr - 1)], p_send)
    drain(turned.at[pl.ds(0, (nc - 1) * F), :], s_send)
    drain(ncs.at[pl.ds(0, nr - 1)], g_send)
    own_t.wait()
    drain(tops.at[pl.ds(0, nc - 1)], t_recv)
    for aa in range(a_count):
        best = tops[4 * aa]
        for yy in range(2):
            for k in range(4):
                best = jnp.maximum(best, tops[yy * 2 * nz + 4 * aa + k])
        here = pl.ds(aa * tile_rows, tile_rows)
        best_out[:, here] = best * inv[:, here]
    drain(tops.at[pl.ds(0, nc - 1)], t_send)


def per_device(nr, nz, embeddings, assigned, centroids):
    nc = 4 * nz
    rows = embeddings.shape[0]
    owned, width = centroids.shape
    a_count = nz // 2
    tile_rows = rows // a_count
    j_count = 256 // nz
    own_rows = rows // nc
    step = min(1024, rows)
    bf, fl = jnp.bfloat16, jnp.float32
    dma = pltpu.SemaphoreType.DMA
    vmem = pl.BlockSpec(memory_space=pltpu.VMEM)
    out, best = pl.pallas_call(
        functools.partial(kernel, nr, nz),
        out_shape=(jax.ShapeDtypeStruct((owned, width), bf), jax.ShapeDtypeStruct((1, rows), fl)),
        in_specs=[vmem] * 3,
        out_specs=(vmem, vmem),
        scratch_shapes=[
            pltpu.VMEM((1, rows), fl),
            pltpu.VMEM((nc, 1, own_rows), fl),
            pltpu.VMEM((1, own_rows), fl),
            pltpu.VMEM((1, rows), fl),
            pltpu.VMEM((nc, F, tile_rows), bf),
            pltpu.VMEM((4 * nr * F, step), bf),
            pltpu.VMEM((4 * nr * F, 256), fl),
            pltpu.VMEM((4 * nr * F, 256), bf),
            pltpu.VMEM((nr, 128, 256), bf),
            pltpu.VMEM((128, 256), bf),
            pltpu.VMEM((width, 128), bf),
            pltpu.VMEM((a_count, j_count, width), bf),
            pltpu.VMEM((nr, 128, width), bf),
            pltpu.VMEM((1, tile_rows), fl),
            pltpu.VMEM((nc, 1, tile_rows), fl),
            dma((8,)), dma, dma, dma, dma, dma, dma, dma((nc,)), dma, dma,
            dma, dma, dma, dma, dma, dma, dma, dma,
        ],
        compiler_params=pltpu.CompilerParams(
            collective_id=0, has_side_effects=True, vmem_limit_bytes=48 * 1024 * 1024),
    )(embeddings.T, assigned.reshape(1, rows), centroids)
    return out, best.reshape(rows)


def solution(mesh):
    nr, nz = mesh.shape["row"], mesh.shape["cent"] // 4
    return jax.shard_map(
        functools.partial(per_device, nr, nz),
        mesh=mesh,
        in_specs=(P("row", "cent"), P("row"), P("cent", None)),
        out_specs=(P("cent", None), P("row")),
        check_vma=False,
    )
```

```python
import functools

import jax
import jax.numpy as jnp
from jax import lax
from jax.experimental import pallas as pl
from jax.experimental.pallas import tpu as pltpu
from jax.sharding import PartitionSpec as P

MESH = pl.DeviceIdType.MESH
F = 32
EPS = 1e-06
CUT = 48


def kernel(nx, nz, x_hbm, id_ref, cent_hbm, nc_out, best_out,
           x_ref, q, qmate, qchip, inv, lanes, lows, e, kr, acc, part, got, summed, zb, turned, centbuf, ncs,
           top, topmate, tops, loc, m_send, m_recv, n_send, n_recv, ez_send, ef_send, e_recv, c_send, c_recv,
           p_send, p_recv, s_send, s_recv, g_send, ga_recv, gb_recv, t_send, t_recv):
    nr = 2 * nx
    nc = 4 * nz
    chips = 2 * nz
    rows = x_ref.shape[1]
    lines = rows // 128
    half = lines // 2
    a_count = nz // 2
    tile_rows = rows // a_count
    tile_lines = tile_rows // 128
    j_count = 256 // nz
    width = nc * F
    r = lax.axis_index("row")
    c = lax.axis_index("cent")
    core = lax.rem(c, 2)
    z = lax.rem(c // 2, nz)
    y = c // (2 * nz)
    chip = c // 2
    a = z // 2
    x = lax.rem(r, nx)
    yh = r // nx

    def cent_id(yy, zz, cc):
        return yy * (2 * nz) + zz * 2 + cc

    core_mate = cent_id(y, z, 1 - core)
    y_mate = cent_id(1 - y, z, core)

    def remote(src, dst, send, recv, row, cent):
        return pltpu.make_async_remote_copy(
            src_ref=src, dst_ref=dst, send_sem=send, recv_sem=recv,
            device_id=(row, cent), device_id_type=MESH)

    def drain(ref, sem):
        pltpu.make_async_copy(ref, ref, sem).wait()

    def span(start, size):
        return pl.ds(pl.multiple_of(start, size), size)

    in_x = pltpu.make_async_copy(x_hbm, x_ref, loc.at[0])
    in_x.start()
    own_c = pltpu.make_async_copy(cent_hbm.at[span(r * j_count, j_count), :], centbuf.at[a], loc.at[1])
    own_c.start()
    barrier = pltpu.get_barrier_semaphore()
    pl.semaphore_signal(barrier, inc=1, device_id=(r, core_mate), device_id_type=MESH)

    @pl.loop(1, chips)
    def _(i):
        d = lax.rem(chip + i, chips) * 2 + core
        pl.semaphore_signal(barrier, inc=1, device_id=(r, d), device_id_type=MESH)

    @pl.loop(1, nr)
    def _(i):
        pl.semaphore_signal(barrier, inc=1, device_id=(lax.rem(r + i, nr), c), device_id_type=MESH)

    ids = id_ref[...]
    cc = ids // (nr * j_count)
    zz = lax.rem(cc // 2, nz)
    lanes[...] = (lax.rem(cc, 2) * 128 + (zz // 2) * j_count + lax.rem(ids, j_count)).astype(jnp.float32)
    lows[...] = (lax.rem(ids, nr * j_count) // j_count * 4 + (cc // (2 * nz)) * 2 + lax.rem(zz, 2)).astype(jnp.float32)

    in_x.wait()

    @pl.loop(0, lines // 8)
    def _(t):
        wide = x_ref[:, span(t * 1024, 1024)].astype(jnp.float32)
        squares = jnp.sum(wide * wide, axis=0, keepdims=True)
        q[span(t * 8, 8), :] = jnp.concatenate([squares[:, k * 128:(k + 1) * 128] for k in range(8)], axis=0)

    pl.semaphore_wait(barrier, 1 + chips - 1 + nr - 1)

    swap_q = remote(q.at[span((1 - core) * half, half), :], qmate, m_send.at[0], m_recv.at[0], r, core_mate)
    swap_q.start()
    own_e = pltpu.make_async_copy(x_ref.at[:, span(a * tile_rows, tile_rows)], e.at[c], loc.at[2])
    own_e.start()
    swap_q.wait()
    qchip[chip] = (q[span(core * half, half), :] + qmate[...]).astype(jnp.bfloat16)

    @pl.loop(1, chips)
    def _(i):
        d = lax.rem(chip + i, chips) * 2 + core
        remote(qchip.at[chip], qchip.at[chip], n_send, n_recv, r, d).start()

    def turned_z(i):
        return lax.rem(z + (i + 1) // 2 * (2 * lax.rem(i, 2) - 1) + nz, nz)

    @pl.loop(1, nz)
    def _(i):
        zz = turned_z(i)
        remote(x_ref.at[:, span((zz // 2) * tile_rows, tile_rows)], e.at[c], ez_send, e_recv.at[c],
               r, cent_id(y, zz, core)).start()

    own_c.wait()

    @pl.loop(1, a_count)
    def _(i):
        remote(centbuf.at[a], centbuf.at[a], c_send, c_recv, r, cent_id(y, lax.rem(z + 2 * i, nz), core)).start()

    def pass_on(piece, to_y):
        if to_y:
            remote(e.at[piece], e.at[piece], ef_send, e_recv.at[piece], r, y_mate).start()
        remote(e.at[piece], e.at[piece], ef_send, e_recv.at[piece], r, core_mate).start()

    def pass_z(i):
        piece = cent_id(y, turned_z(i), core)
        drain(e.at[piece], e_recv.at[piece])
        pass_on(piece, True)

    def pass_y(i):
        piece = cent_id(1 - y, lax.rem(z + i, nz), core)
        drain(e.at[piece], e_recv.at[piece])
        pass_on(piece, False)

    own_e.wait()
    pass_on(c, True)

    drain(qchip.at[pl.ds(0, chips - 1)], n_recv)
    squares = qchip[0].astype(jnp.float32)
    for i in range(1, chips):
        squares = squares + qchip[i].astype(jnp.float32)
    own_inv = inv.at[span(core * half, half), :]
    own_inv[...] = lax.rsqrt(squares + EPS)
    swap_i = remote(own_inv, own_inv, m_send.at[1], m_recv.at[1], r, core_mate)
    swap_i.start()
    swap_i.wait()

    acc[...] = jnp.zeros_like(acc)
    klo_count = 4 * nr

    def along(block):
        return jnp.concatenate([block[k:k + 1, :] for k in range(8)], axis=1)

    @pl.loop(0, lines // 8)
    def _(t):
        own8 = span(t * 8, 8)
        scale = along(inv[own8, :])
        unit = (x_ref[:, span(t * 1024, 1024)].astype(jnp.float32) * scale).astype(jnp.bfloat16)
        lane_b = jnp.broadcast_to(along(lanes[own8, :]), (256, 1024)).astype(jnp.bfloat16)
        iota = lax.broadcasted_iota(jnp.int32, (256, 1024), 0).astype(jnp.float32).astype(jnp.bfloat16)
        one = jnp.bfloat16(1)
        nil = jnp.bfloat16(0)
        hot = jnp.where(lane_b == iota, one, nil)
        low_b = jnp.broadcast_to(along(lows[own8, :]), (F, 1024)).astype(jnp.bfloat16)
        for j in range(klo_count):
            kr[j * F:(j + 1) * F, :] = jnp.where(low_b == jnp.bfloat16(j), unit, nil)
        acc[...] += lax.dot_general(kr[...], hot, (((1,), (1,)), ((), ())), preferred_element_type=jnp.float32)

    part[...] = acc[...].astype(jnp.bfloat16)

    @pl.loop(1, nr)
    def _(i):
        rr = lax.rem(r + i, nr)
        remote(part.at[span(rr * 128, 128), :], got.at[r], p_send, p_recv, rr, c).start()

    got[r] = part[span(r * 128, 128), :]

    first_pass = 3 * nz // 4 + 1

    @pl.loop(1, first_pass)
    def _(i):
        pass_z(i)

    drain(got.at[pl.ds(0, nr - 1)], p_recv)
    total = got[0].astype(jnp.float32)
    for i in range(1, nr):
        total = total + got[i].astype(jnp.float32)
    summed[...] = total.astype(jnp.bfloat16).reshape(4, F, 256)

    swap_s = remote(summed.at[:, :, span((1 - core) * 128, 128)], zb.at[:, span(core * F, F), :],
                    m_send.at[2], m_recv.at[2], r, core_mate)
    swap_s.start()
    zb[:, span(core * F, F), :] = summed[:, :, span(core * 128, 128)]
    swap_s.wait()

    @pl.loop(1, chips)
    def _(i):
        d = lax.rem(chip + i, chips)
        remote(zb.at[d // nz * 2 + lax.rem(d, 2)], turned.at[span(chip * 2 * F, 2 * F), :], s_send, s_recv,
               r, d * 2 + core).start()

    turned[span(chip * 2 * F, 2 * F), :] = zb[y * 2 + lax.rem(z, 2)]
    if a_count > 1:
        drain(centbuf.at[pl.ds(0, a_count - 1)], c_recv)

    @pl.loop(first_pass, nz)
    def _(i):
        pass_z(i)

    drain(turned.at[pl.ds(0, (chips - 1) * 2 * F), :], s_recv)
    fresh = turned[...].astype(jnp.float32).T + centbuf[...].reshape(128, width).astype(jnp.float32)
    fresh = fresh * lax.rsqrt(jnp.sum(fresh * fresh, axis=1, keepdims=True) + EPS)
    ncs[r] = fresh.astype(jnp.bfloat16)

    def pa(slot):
        return ncs.at[slot, pl.ds(0, CUT), :]

    def pb(slot):
        return ncs.at[slot, pl.ds(CUT, 128 - CUT), :]

    other = (1 - yh) * nx + x
    remote(pa(r), pa(r), g_send, ga_recv.at[r], other, c).start()
    for i in range(1, nx):
        mate = yh * nx + lax.rem(x + i, nx)
        remote(pb(r), pb(r), g_send, gb_recv.at[r], mate, c).start()
    for i in range(1, nx):
        mate = yh * nx + lax.rem(x + i, nx)
        remote(pa(r), pa(r), g_send, ga_recv.at[r], mate, c).start()
    remote(pb(r), pb(r), g_send, gb_recv.at[r], other, c).start()
    drain(pa(other), ga_recv.at[other])
    for i in range(1, nx):
        mate = yh * nx + lax.rem(x + i, nx)
        remote(pa(other), pa(other), g_send, ga_recv.at[other], mate, c).start()
    for i in range(1, nx):
        near = yh * nx + lax.rem(x + i, nx)
        drain(pb(near), gb_recv.at[near])
        remote(pb(near), pb(near), g_send, gb_recv.at[near], other, c).start()

    @pl.loop(0, nz)
    def _(i):
        pass_y(i)

    @pl.loop(0, 2 * nz)
    def _(i):
        piece = cent_id(i // nz, lax.rem(i, nz), 1 - core)
        drain(e.at[piece], e_recv.at[piece])

    for i in range(1, nx):
        near = yh * nx + lax.rem(x + i, nx)
        drain(pa(near), ga_recv.at[near])

    wide_rows = 256

    def score(first_slot, merge):
        block = ncs[pl.ds(first_slot, nx)].reshape(nx * 128, width)

        @pl.loop(0, tile_rows // wide_rows)
        def _(t):
            here = span(t * wide_rows, wide_rows)
            scores = jnp.dot(block, e[:, :, here].reshape(width, wide_rows), preferred_element_type=jnp.float32)
            best = jnp.max(scores, axis=0, keepdims=True)
            for k in range(2):
                line = pl.ds(t * 2 + k, 1)
                piece = best[:, k * 128:(k + 1) * 128]
                top[line, :] = jnp.maximum(top[line, :], piece) if merge else piece

    score(yh * nx, False)

    for i in range(1, nx):
        far = (1 - yh) * nx + lax.rem(x + i, nx)
        drain(pa(far), ga_recv.at[far])
        drain(pb(far), gb_recv.at[far])
    drain(pb(other), gb_recv.at[other])

    score((1 - yh) * nx, True)

    own_half = tile_lines // 2
    swap_t = remote(top.at[span((1 - core) * own_half, own_half), :], topmate, m_send.at[3], m_recv.at[3], r, core_mate)
    swap_t.start()
    for i in range(nr):
        nc_out[i * j_count:(i + 1) * j_count, :] = ncs[i, span(a * j_count, j_count), :]
    swap_t.wait()
    tops[chip] = jnp.maximum(top[span(core * own_half, own_half), :], topmate[...])

    @pl.loop(1, chips)
    def _(i):
        d = lax.rem(chip + i, chips) * 2 + core
        remote(tops.at[chip], tops.at[chip], t_send, t_recv, r, d).start()

    drain(qchip.at[pl.ds(0, chips - 1)], n_send)
    drain(e.at[pl.ds(0, nz - 1)], ez_send)
    drain(e.at[pl.ds(0, 3 * nz)], ef_send)
    if a_count > 1:
        drain(centbuf.at[pl.ds(0, a_count - 1)], c_send)
    drain(got.at[pl.ds(0, nr - 1)], p_send)
    drain(turned.at[pl.ds(0, (chips - 1) * 2 * F), :], s_send)
    drain(ncs.at[pl.ds(0, nr - 1)], g_send)

    drain(tops.at[pl.ds(0, chips - 1)], t_recv)
    for aa in range(a_count):
        best = tops[2 * aa]
        for yy in range(2):
            for k in range(2):
                best = jnp.maximum(best, tops[yy * nz + 2 * aa + k])
        first = aa * tile_lines
        here = span(first + core * own_half, own_half)
        best_out[here, :] = best * inv[here, :]
        there = best_out.at[here, :]
        remote(there, there, m_send.at[4], m_recv.at[4], r, core_mate).start()
    drain(best_out.at[pl.ds(0, half), :], m_recv.at[4])
    drain(best_out.at[pl.ds(0, half), :], m_send.at[4])
    drain(tops.at[pl.ds(0, chips - 1)], t_send)


def per_device(nx, nz, embeddings, assigned, centroids):
    nr, nc, chips = 2 * nx, 4 * nz, 2 * nz
    rows = embeddings.shape[0]
    owned, width = centroids.shape
    a_count = nz // 2
    tile_rows = rows // a_count
    lines = rows // 128
    j_count = 256 // nz
    bf, fl = jnp.bfloat16, jnp.float32
    dma = pltpu.SemaphoreType.DMA
    vmem = pl.BlockSpec(memory_space=pltpu.VMEM)
    hbm = pl.BlockSpec(memory_space=pltpu.HBM)
    out, best = pl.pallas_call(
        functools.partial(kernel, nx, nz),
        out_shape=(jax.ShapeDtypeStruct((owned, width), bf), jax.ShapeDtypeStruct((lines, 128), fl)),
        in_specs=[hbm, vmem, hbm],
        out_specs=(vmem, vmem),
        scratch_shapes=[
            pltpu.VMEM((F, rows), bf),
            pltpu.VMEM((lines, 128), fl),
            pltpu.VMEM((lines // 2, 128), fl),
            pltpu.VMEM((chips, lines // 2, 128), bf),
            pltpu.VMEM((lines, 128), fl),
            pltpu.VMEM((lines, 128), fl),
            pltpu.VMEM((lines, 128), fl),
            pltpu.VMEM((nc, F, tile_rows), bf),
            pltpu.VMEM((4 * nr * F, 1024), bf),
            pltpu.VMEM((4 * nr * F, 256), fl),
            pltpu.VMEM((4 * nr * F, 256), bf),
            pltpu.VMEM((nr, 128, 256), bf),
            pltpu.VMEM((4, F, 256), bf),
            pltpu.VMEM((4, 2 * F, 128), bf),
            pltpu.VMEM((width, 128), bf),
            pltpu.VMEM((a_count, j_count, width), bf),
            pltpu.VMEM((nr, 128, width), bf),
            pltpu.VMEM((tile_rows // 128, 128), fl),
            pltpu.VMEM((tile_rows // 256, 128), fl),
            pltpu.VMEM((chips, tile_rows // 256, 128), fl),
            dma((4,)), dma((5,)), dma((5,)), dma, dma, dma, dma, dma((nc,)), dma, dma,
            dma, dma, dma, dma, dma, dma((nr,)), dma((nr,)), dma, dma,
        ],
        compiler_params=pltpu.CompilerParams(
            collective_id=0, has_side_effects=True, vmem_limit_bytes=48 * 1024 * 1024),
    )(embeddings.T, assigned.reshape(lines, 128), centroids)
    return out, best.reshape(rows)


def solution(mesh):
    nx, nz = mesh.shape["row"] // 2, mesh.shape["cent"] // 4
    return jax.shard_map(
        functools.partial(per_device, nx, nz),
        mesh=mesh,
        in_specs=(P("row", "cent"), P("row"), P("cent", None)),
        out_specs=(P("cent", None), P("row")),
        check_vma=False,
    )
```

```python
import functools

import jax
import jax.numpy as jnp
from jax import lax
from jax.experimental import pallas as pl
from jax.experimental.pallas import tpu as pltpu
from jax.sharding import PartitionSpec as P

MESH = pl.DeviceIdType.MESH
F = 32
EPS = 1e-06
FIRST = 6
CUT = 64
TILE = 1024


def kernel(nx, nz, x_hbm, id_ref, cent_hbm, nc_out, best_out,
           x_ref, q, qmate, qchip, inv, lanes, lows, e, kr, acc, part, got, summed, zb, turned, centbuf, ncs,
           top, topmate, tops, loc, m_send, m_recv, n_send, n_recv, ez_send, ef_send, e_recv, c_send, c_recv,
           p_send, p_recv, s_send, s_recv, g_send, g_recv, t_send, t_recv):
    nr = 2 * nx
    nc = 4 * nz
    chips = 2 * nz
    rows = x_ref.shape[1]
    lines = rows // 128
    half = lines // 2
    a_count = nz // 2
    tile_rows = rows // a_count
    tile_lines = tile_rows // 128
    j_count = 256 // nz
    width = nc * F
    r = lax.axis_index("row")
    c = lax.axis_index("cent")
    core = lax.rem(c, 2)
    z = lax.rem(c // 2, nz)
    y = c // (2 * nz)
    chip = c // 2
    a = z // 2
    x = lax.rem(r, nx)
    yh = r // nx

    def cent_id(yy, zz, cc):
        return yy * (2 * nz) + zz * 2 + cc

    core_mate = cent_id(y, z, 1 - core)
    y_mate = cent_id(1 - y, z, core)

    def remote(src, dst, send, recv, row, cent):
        return pltpu.make_async_remote_copy(
            src_ref=src, dst_ref=dst, send_sem=send, recv_sem=recv,
            device_id=(row, cent), device_id_type=MESH)

    def drain(ref, sem):
        pltpu.make_async_copy(ref, ref, sem).wait()

    def span(start, size):
        return pl.ds(pl.multiple_of(start, size), size)

    in_x = pltpu.make_async_copy(x_hbm, x_ref, loc.at[0])
    in_x.start()
    own_c = pltpu.make_async_copy(cent_hbm.at[span(r * j_count, j_count), :], centbuf.at[a], loc.at[1])
    own_c.start()
    barrier = pltpu.get_barrier_semaphore()
    pl.semaphore_signal(barrier, inc=1, device_id=(r, core_mate), device_id_type=MESH)

    @pl.loop(1, chips)
    def _(i):
        d = lax.rem(chip + i, chips) * 2 + core
        pl.semaphore_signal(barrier, inc=1, device_id=(r, d), device_id_type=MESH)

    @pl.loop(1, nr)
    def _(i):
        pl.semaphore_signal(barrier, inc=1, device_id=(lax.rem(r + i, nr), c), device_id_type=MESH)

    ids = id_ref[...]
    cc = ids // (nr * j_count)
    zz = lax.rem(cc // 2, nz)
    lanes[...] = (lax.rem(cc, 2) * 128 + (zz // 2) * j_count + lax.rem(ids, j_count)).astype(jnp.float32)
    lows[...] = (lax.rem(ids, nr * j_count) // j_count * 4 + (cc // (2 * nz)) * 2 + lax.rem(zz, 2)).astype(jnp.float32)

    in_x.wait()

    @pl.loop(0, lines // 8)
    def _(t):
        wide = x_ref[:, span(t * 1024, 1024)].astype(jnp.float32)
        squares = jnp.sum(wide * wide, axis=0, keepdims=True)
        q[span(t * 8, 8), :] = jnp.concatenate([squares[:, k * 128:(k + 1) * 128] for k in range(8)], axis=0)

    pl.semaphore_wait(barrier, 1 + chips - 1 + nr - 1)

    swap_q = remote(q.at[span((1 - core) * half, half), :], qmate, m_send.at[0], m_recv.at[0], r, core_mate)
    swap_q.start()
    own_e = pltpu.make_async_copy(x_ref.at[:, span(a * tile_rows, tile_rows)], e.at[c], loc.at[2])
    own_e.start()
    swap_q.wait()
    qchip[chip] = (q[span(core * half, half), :] + qmate[...]).astype(jnp.bfloat16)

    @pl.loop(1, chips)
    def _(i):
        d = lax.rem(chip + i, chips) * 2 + core
        remote(qchip.at[chip], qchip.at[chip], n_send, n_recv, r, d).start()

    outward = 2 * lax.rem(z, 2) - 1

    def at_z(steps):
        return lax.rem(z + outward * steps + nz, nz)

    z_mate = cent_id(y, at_z(-1), core)
    direct = (1, 2, 3) if nz == 8 else ()
    for steps in (-1, 1, -2, 3) if nz == 8 else (-1,):
        to = at_z(steps)
        remote(x_ref.at[:, span((to // 2) * tile_rows, tile_rows)], e.at[c], ez_send, e_recv.at[c],
               r, cent_id(y, to, core)).start()

    own_c.wait()

    @pl.loop(1, a_count)
    def _(i):
        remote(centbuf.at[a], centbuf.at[a], c_send, c_recv, r, cent_id(y, lax.rem(z + 2 * i, nz), core)).start()

    def pass_on(piece, to_z, to_y):
        if to_z:
            remote(e.at[piece], e.at[piece], ef_send, e_recv.at[piece], r, z_mate).start()
        if to_y:
            remote(e.at[piece], e.at[piece], ef_send, e_recv.at[piece], r, y_mate).start()
        remote(e.at[piece], e.at[piece], ef_send, e_recv.at[piece], r, core_mate).start()

    def pass_z(steps):
        piece = cent_id(y, at_z(steps), core)
        drain(e.at[piece], e_recv.at[piece])
        pass_on(piece, steps > 0, True)

    def pass_y(steps):
        piece = cent_id(1 - y, at_z(steps), core)
        drain(e.at[piece], e_recv.at[piece])
        pass_on(piece, False, False)

    order = (0, -1, 1, -2, 2, 3, -3, -4) if nz == 8 else (0, -1)

    own_e.wait()
    pass_on(c, False, True)

    drain(qchip.at[pl.ds(0, chips - 1)], n_recv)
    squares = qchip[0].astype(jnp.float32)
    for i in range(1, chips):
        squares = squares + qchip[i].astype(jnp.float32)
    own_inv = inv.at[span(core * half, half), :]
    own_inv[...] = lax.rsqrt(squares + EPS)
    swap_i = remote(own_inv, own_inv, m_send.at[1], m_recv.at[1], r, core_mate)
    swap_i.start()
    swap_i.wait()

    acc[...] = jnp.zeros_like(acc)
    klo_count = 4 * nr

    def along(block):
        return jnp.concatenate([block[k:k + 1, :] for k in range(8)], axis=1)

    @pl.loop(0, lines // 8)
    def _(t):
        own8 = span(t * 8, 8)
        scale = along(inv[own8, :])
        unit = (x_ref[:, span(t * 1024, 1024)].astype(jnp.float32) * scale).astype(jnp.bfloat16)
        lane_b = jnp.broadcast_to(along(lanes[own8, :]), (256, 1024)).astype(jnp.bfloat16)
        iota = lax.broadcasted_iota(jnp.int32, (256, 1024), 0).astype(jnp.float32).astype(jnp.bfloat16)
        one = jnp.bfloat16(1)
        nil = jnp.bfloat16(0)
        hot = jnp.where(lane_b == iota, one, nil)
        low_b = jnp.broadcast_to(along(lows[own8, :]), (F, 1024)).astype(jnp.bfloat16)
        for j in range(klo_count):
            kr[j * F:(j + 1) * F, :] = jnp.where(low_b == jnp.bfloat16(j), unit, nil)
        acc[...] += lax.dot_general(kr[...], hot, (((1,), (1,)), ((), ())), preferred_element_type=jnp.float32)

    part[...] = acc[...].astype(jnp.bfloat16)

    @pl.loop(1, nr)
    def _(i):
        rr = lax.rem(r + i, nr)
        remote(part.at[span(rr * 128, 128), :], got.at[r], p_send, p_recv, rr, c).start()

    got[r] = part[span(r * 128, 128), :]

    for steps in order[1:FIRST]:
        pass_z(steps)

    drain(got.at[pl.ds(0, nr - 1)], p_recv)
    total = got[0].astype(jnp.float32)
    for i in range(1, nr):
        total = total + got[i].astype(jnp.float32)
    summed[...] = total.astype(jnp.bfloat16).reshape(4, F, 256)

    swap_s = remote(summed.at[:, :, span((1 - core) * 128, 128)], zb.at[:, span(core * F, F), :],
                    m_send.at[2], m_recv.at[2], r, core_mate)
    swap_s.start()
    zb[:, span(core * F, F), :] = summed[:, :, span(core * 128, 128)]
    swap_s.wait()

    @pl.loop(1, chips)
    def _(i):
        d = lax.rem(chip + i, chips)
        remote(zb.at[d // nz * 2 + lax.rem(d, 2)], turned.at[span(chip * 2 * F, 2 * F), :], s_send, s_recv,
               r, d * 2 + core).start()

    turned[span(chip * 2 * F, 2 * F), :] = zb[y * 2 + lax.rem(z, 2)]
    if a_count > 1:
        drain(centbuf.at[pl.ds(0, a_count - 1)], c_recv)

    for steps in order[FIRST:]:
        pass_z(steps)

    for steps in order[:nz // 2]:
        pass_y(steps)

    drain(turned.at[pl.ds(0, (chips - 1) * 2 * F), :], s_recv)
    fresh = turned[...].astype(jnp.float32).T + centbuf[...].reshape(128, width).astype(jnp.float32)
    fresh = fresh * lax.rsqrt(jnp.sum(fresh * fresh, axis=1, keepdims=True) + EPS)
    ncs[0] = fresh.astype(jnp.bfloat16)

    up = yh * nx + lax.rem(x + 1, nx)
    down = yh * nx + lax.rem(x + nx - 1, nx)
    over = (1 - yh) * nx + x

    def cut(part, side):
        first, size = ((0, CUT), (CUT, 128 - CUT))[part]
        if side is None:
            return pl.ds(first, size)
        return pl.ds(first + side * (size // 2), size // 2)

    def push(slot, to, part, side, target):
        kind = part * 3 + (0 if side is None else 1 + side)
        rows_of = cut(part, side)
        remote(ncs.at[slot, rows_of, :], ncs.at[to, rows_of, :], g_send, g_recv.at[to, kind], target, c).start()

    def arrive(slot, part, side):
        kind = part * 3 + (0 if side is None else 1 + side)
        ref = ncs.at[slot, cut(part, side), :]
        drain(ref, g_recv.at[slot, kind])

    ring = nx == 4

    def round_x(base, part):
        push(base, base + nx - 1, part, None, up)
        if ring:
            push(base, base + 1, part, None, down)

    def relay(base, part, also):
        arrive(base + nx - 1, part, None)
        if ring:
            push(base + 3, base + 2, part, 0, up)
        if also:
            push(base + nx - 1, nx + base + nx - 1, part, None, over)
        if ring:
            arrive(base + 1, part, None)
            push(base + 1, base + 2, part, 1, down)
            if also:
                push(base + 1, nx + base + 1, part, None, over)

    push(0, nx, 0, None, over)
    round_x(0, 1)
    round_x(0, 0)
    push(0, nx, 1, None, over)
    relay(0, 1, True)
    arrive(nx, 0, None)
    round_x(nx, 0)
    relay(0, 0, False)
    if ring:
        for side in range(2):
            arrive(2, 1, side)
            push(2, nx + 2, 1, side, over)

    for steps in order[nz // 2:]:
        pass_y(steps)

    relay(nx, 0, False)

    @pl.loop(0, 2 * nz)
    def _(i):
        piece = cent_id(i // nz, lax.rem(i, nz), 1 - core)
        drain(e.at[piece], e_recv.at[piece])

    if ring:
        for side in range(2):
            arrive(2, 0, side)
    arrive(nx, 1, None)

    def score(first_slot, slots, merge):
        block = ncs[first_slot:first_slot + slots].reshape(slots * 128, width)

        @pl.loop(0, tile_rows // TILE)
        def _(t):
            here = span(t * TILE, TILE)
            scores = jnp.dot(block, e[:, :, here].reshape(width, TILE), preferred_element_type=jnp.float32)
            best = jnp.max(scores, axis=0, keepdims=True)
            for k in range(TILE // 128):
                line = pl.ds(t * (TILE // 128) + k, 1)
                piece = best[:, k * 128:(k + 1) * 128]
                top[line, :] = jnp.maximum(top[line, :], piece) if merge else piece

    score(0, nx + 1, False)

    arrive(nx + nx - 1, 1, None)
    if ring:
        arrive(nx + 1, 1, None)
        for side in range(2):
            arrive(nx + 2, 0, side)
            arrive(nx + 2, 1, side)

    score(nx + 1, nx - 1, True)

    own_half = tile_lines // 2
    swap_t = remote(top.at[span((1 - core) * own_half, own_half), :], topmate, m_send.at[3], m_recv.at[3], r, core_mate)
    swap_t.start()
    for i in range(nr):
        row = (yh if i < nx else 1 - yh) * nx + lax.rem(x + i, nx)
        nc_out[span(row * j_count, j_count), :] = ncs[i, span(a * j_count, j_count), :]
    swap_t.wait()
    tops[chip] = jnp.maximum(top[span(core * own_half, own_half), :], topmate[...])

    @pl.loop(1, chips)
    def _(i):
        d = lax.rem(chip + i, chips) * 2 + core
        remote(tops.at[chip], tops.at[chip], t_send, t_recv, r, d).start()

    drain(qchip.at[pl.ds(0, chips - 1)], n_send)
    drain(e.at[pl.ds(0, 1 + len(direct))], ez_send)
    drain(e.at[pl.ds(0, 3 * nz + len(direct))], ef_send)
    if a_count > 1:
        drain(centbuf.at[pl.ds(0, a_count - 1)], c_send)
    drain(got.at[pl.ds(0, nr - 1)], p_send)
    drain(turned.at[pl.ds(0, (chips - 1) * 2 * F), :], s_send)
    drain(ncs.at[pl.ds(0, nr - 1)], g_send)

    drain(tops.at[pl.ds(0, chips - 1)], t_recv)
    for aa in range(a_count):
        best = tops[2 * aa]
        for yy in range(2):
            for k in range(2):
                best = jnp.maximum(best, tops[yy * nz + 2 * aa + k])
        first = aa * tile_lines
        here = span(first + core * own_half, own_half)
        best_out[here, :] = best * inv[here, :]
        there = best_out.at[here, :]
        remote(there, there, m_send.at[4], m_recv.at[4], r, core_mate).start()
    drain(best_out.at[pl.ds(0, half), :], m_recv.at[4])
    drain(best_out.at[pl.ds(0, half), :], m_send.at[4])
    drain(tops.at[pl.ds(0, chips - 1)], t_send)


def per_device(nx, nz, embeddings, assigned, centroids):
    nr, nc, chips = 2 * nx, 4 * nz, 2 * nz
    rows = embeddings.shape[0]
    owned, width = centroids.shape
    a_count = nz // 2
    tile_rows = rows // a_count
    lines = rows // 128
    j_count = 256 // nz
    bf, fl = jnp.bfloat16, jnp.float32
    dma = pltpu.SemaphoreType.DMA
    vmem = pl.BlockSpec(memory_space=pltpu.VMEM)
    hbm = pl.BlockSpec(memory_space=pltpu.HBM)
    out, best = pl.pallas_call(
        functools.partial(kernel, nx, nz),
        out_shape=(jax.ShapeDtypeStruct((owned, width), bf), jax.ShapeDtypeStruct((lines, 128), fl)),
        in_specs=[hbm, vmem, hbm],
        out_specs=(vmem, vmem),
        scratch_shapes=[
            pltpu.VMEM((F, rows), bf),
            pltpu.VMEM((lines, 128), fl),
            pltpu.VMEM((lines // 2, 128), fl),
            pltpu.VMEM((chips, lines // 2, 128), bf),
            pltpu.VMEM((lines, 128), fl),
            pltpu.VMEM((lines, 128), fl),
            pltpu.VMEM((lines, 128), fl),
            pltpu.VMEM((nc, F, tile_rows), bf),
            pltpu.VMEM((4 * nr * F, 1024), bf),
            pltpu.VMEM((4 * nr * F, 256), fl),
            pltpu.VMEM((4 * nr * F, 256), bf),
            pltpu.VMEM((nr, 128, 256), bf),
            pltpu.VMEM((4, F, 256), bf),
            pltpu.VMEM((4, 2 * F, 128), bf),
            pltpu.VMEM((width, 128), bf),
            pltpu.VMEM((a_count, j_count, width), bf),
            pltpu.VMEM((nr, 128, width), bf),
            pltpu.VMEM((tile_rows // 128, 128), fl),
            pltpu.VMEM((tile_rows // 256, 128), fl),
            pltpu.VMEM((chips, tile_rows // 256, 128), fl),
            dma((4,)), dma((5,)), dma((5,)), dma, dma, dma, dma, dma((nc,)), dma, dma,
            dma, dma, dma, dma, dma, dma((nr, 6)), dma, dma,
        ],
        compiler_params=pltpu.CompilerParams(
            collective_id=0, has_side_effects=True, vmem_limit_bytes=48 * 1024 * 1024),
    )(embeddings.T, assigned.reshape(lines, 128), centroids)
    return out, best.reshape(rows)


def solution(mesh):
    nx, nz = mesh.shape["row"] // 2, mesh.shape["cent"] // 4
    return jax.shard_map(
        functools.partial(per_device, nx, nz),
        mesh=mesh,
        in_specs=(P("row", "cent"), P("row"), P("cent", None)),
        out_specs=(P("cent", None), P("row")),
        check_vma=False,
    )
```

```python
import functools

import jax
import jax.numpy as jnp
from jax import lax
from jax.experimental import pallas as pl
from jax.experimental.pallas import tpu as pltpu
from jax.sharding import PartitionSpec as P

MESH = pl.DeviceIdType.MESH
F = 32
EPS = 1e-06
CUT = 64
TILE = 1024


def kernel(nx, nz, x_hbm, id_ref, cent_hbm, nc_out, best_out,
           x_ref, q, qmate, qchip, inv, lanes, lows, hot, unit, e, kr, acc, part, got, summed, zb, turned, centbuf, ncs,
           top, topmate, tops, loc, m_send, m_recv, n_send, n_recv, ez_send, ef_send, e_recv, c_send, c_recv,
           p_send, p_recv, s_send, s_recv, g_send, g_recv, t_send, t_recv):
    nr = 2 * nx
    nc = 4 * nz
    chips = 2 * nz
    rows = x_ref.shape[1]
    lines = rows // 128
    half = lines // 2
    a_count = nz // 2
    tile_rows = rows // a_count
    tile_lines = tile_rows // 128
    j_count = 256 // nz
    width = nc * F
    r = lax.axis_index("row")
    c = lax.axis_index("cent")
    core = lax.rem(c, 2)
    z = lax.rem(c // 2, nz)
    y = c // (2 * nz)
    chip = c // 2
    a = z // 2
    x = lax.rem(r, nx)
    yh = r // nx

    def cent_id(yy, zz, cc):
        return yy * (2 * nz) + zz * 2 + cc

    core_mate = cent_id(y, z, 1 - core)
    y_mate = cent_id(1 - y, z, core)

    def remote(src, dst, send, recv, row, cent):
        return pltpu.make_async_remote_copy(
            src_ref=src, dst_ref=dst, send_sem=send, recv_sem=recv,
            device_id=(row, cent), device_id_type=MESH)

    def drain(ref, sem):
        pltpu.make_async_copy(ref, ref, sem).wait()

    def span(start, size):
        return pl.ds(pl.multiple_of(start, size), size)

    in_x = pltpu.make_async_copy(x_hbm, x_ref, loc.at[0])
    in_x.start()
    own_c = pltpu.make_async_copy(cent_hbm.at[span(r * j_count, j_count), :], centbuf.at[a], loc.at[1])
    own_c.start()
    barrier = pltpu.get_barrier_semaphore()
    pl.semaphore_signal(barrier, inc=1, device_id=(r, core_mate), device_id_type=MESH)

    @pl.loop(1, chips)
    def _(i):
        d = lax.rem(chip + i, chips) * 2 + core
        pl.semaphore_signal(barrier, inc=1, device_id=(r, d), device_id_type=MESH)

    @pl.loop(1, nr)
    def _(i):
        pl.semaphore_signal(barrier, inc=1, device_id=(lax.rem(r + i, nr), c), device_id_type=MESH)

    ids = id_ref[...]
    cc = ids // (nr * j_count)
    zz = lax.rem(cc // 2, nz)
    lanes[...] = (lax.rem(cc, 2) * 128 + (zz // 2) * j_count + lax.rem(ids, j_count)).astype(jnp.float32)
    ahead = lax.rem(lax.rem(ids, nr * j_count) // j_count + (2 * nr - 1) - r, nr)
    lows[...] = (ahead * 4 + (cc // (2 * nz)) * 2 + lax.rem(zz, 2)).astype(jnp.float32)

    in_x.wait()

    @pl.loop(0, lines // 8)
    def _(t):
        wide = x_ref[:, span(t * 1024, 1024)].astype(jnp.float32)
        squares = jnp.sum(wide * wide, axis=0, keepdims=True)
        q[span(t * 8, 8), :] = jnp.concatenate([squares[:, k * 128:(k + 1) * 128] for k in range(8)], axis=0)

    pl.semaphore_wait(barrier, 1 + chips - 1 + nr - 1)

    swap_q = remote(q.at[span((1 - core) * half, half), :], qmate, m_send.at[0], m_recv.at[0], r, core_mate)
    swap_q.start()
    own_e = pltpu.make_async_copy(x_ref.at[:, span(a * tile_rows, tile_rows)], e.at[c], loc.at[2])
    own_e.start()
    swap_q.wait()
    qchip[chip] = (q[span(core * half, half), :] + qmate[...]).astype(jnp.bfloat16)

    @pl.loop(1, chips)
    def _(i):
        d = lax.rem(chip + i, chips) * 2 + core
        remote(qchip.at[chip], qchip.at[chip], n_send, n_recv, r, d).start()

    outward = 2 * lax.rem(z, 2) - 1

    def at_z(steps):
        return lax.rem(z + outward * steps + nz, nz)

    z_mate = cent_id(y, at_z(-1), core)
    direct = (1, 2, 3) if nz == 8 else ()
    for steps in (-1, 1, -2, 3) if nz == 8 else (-1,):
        to = at_z(steps)
        remote(x_ref.at[:, span((to // 2) * tile_rows, tile_rows)], e.at[c], ez_send, e_recv.at[c],
               r, cent_id(y, to, core)).start()

    own_c.wait()

    @pl.loop(1, a_count)
    def _(i):
        remote(centbuf.at[a], centbuf.at[a], c_send, c_recv, r, cent_id(y, lax.rem(z + 2 * i, nz), core)).start()

    def pass_on(piece, to_z, to_y):
        if to_z:
            remote(e.at[piece], e.at[piece], ef_send, e_recv.at[piece], r, z_mate).start()
        if to_y:
            remote(e.at[piece], e.at[piece], ef_send, e_recv.at[piece], r, y_mate).start()
        remote(e.at[piece], e.at[piece], ef_send, e_recv.at[piece], r, core_mate).start()

    def pass_z(steps):
        piece = cent_id(y, at_z(steps), core)
        drain(e.at[piece], e_recv.at[piece])
        pass_on(piece, steps > 0, steps > 0)

    def pass_y(steps):
        piece = cent_id(1 - y, at_z(steps), core)
        drain(e.at[piece], e_recv.at[piece])
        pass_on(piece, steps >= 0, False)

    near, far = ((0, 1, 2, 3), (-1, -2, -3, -4)) if nz == 8 else ((0,), (-1,))

    own_e.wait()
    pass_on(c, False, True)

    def along(block):
        return jnp.concatenate([block[k:k + 1, :] for k in range(8)], axis=1)

    @pl.loop(0, lines // 8)
    def _(t):
        lane_b = jnp.broadcast_to(along(lanes[span(t * 8, 8), :]), (256, 1024)).astype(jnp.bfloat16)
        iota = lax.broadcasted_iota(jnp.int32, (256, 1024), 0).astype(jnp.float32).astype(jnp.bfloat16)
        hot[:, span(t * 1024, 1024)] = jnp.where(lane_b == iota, jnp.bfloat16(1), jnp.bfloat16(0))

    drain(qchip.at[pl.ds(0, chips - 1)], n_recv)
    squares = qchip[0].astype(jnp.float32)
    for i in range(1, chips):
        squares = squares + qchip[i].astype(jnp.float32)
    own_inv = inv.at[span(core * half, half), :]
    own_inv[...] = lax.rsqrt(squares + EPS)
    swap_i = remote(own_inv, own_inv, m_send.at[1], m_recv.at[1], r, core_mate)
    swap_i.start()
    swap_i.wait()

    group = nr // 2
    block_rows = 4 * F

    @pl.loop(0, lines // 8)
    def _(t):
        here = span(t * 1024, 1024)
        unit[:, here] = (x_ref[:, here].astype(jnp.float32) * along(inv[span(t * 8, 8), :])).astype(jnp.bfloat16)

    for g in range(2):
        @pl.loop(0, lines // 8)
        def _(t):
            here = span(t * 1024, 1024)
            low_b = jnp.broadcast_to(along(lows[span(t * 8, 8), :]), (F, 1024)).astype(jnp.bfloat16)
            mine = unit[:, here]
            for j in range(4 * group):
                kr[j * F:(j + 1) * F, :] = jnp.where(low_b == jnp.bfloat16(g * 4 * group + j), mine, jnp.bfloat16(0))
            product = lax.dot_general(kr[...], hot[:, here], (((1,), (1,)), ((), ())), preferred_element_type=jnp.float32)

            @pl.when(t == 0)
            def _():
                acc[...] = product

            @pl.when(t > 0)
            def _():
                acc[...] += product

        part[g * group * block_rows:(g + 1) * group * block_rows, :] = acc[...].astype(jnp.bfloat16)
        for k in range(g * group, (g + 1) * group):
            if k < nr - 1:
                remote(part.at[pl.ds(k * block_rows, block_rows), :], got.at[r], p_send, p_recv,
                       lax.rem(r + 1 + k, nr), c).start()

    got[r] = part[(nr - 1) * block_rows:, :]

    for steps in near[1:]:
        pass_z(steps)

    drain(got.at[pl.ds(0, nr - 1)], p_recv)
    total = got[0].astype(jnp.float32)
    for i in range(1, nr):
        total = total + got[i].astype(jnp.float32)
    summed[...] = total.astype(jnp.bfloat16).reshape(4, F, 256)

    swap_s = remote(summed.at[:, :, span((1 - core) * 128, 128)], zb.at[:, span(core * F, F), :],
                    m_send.at[2], m_recv.at[2], r, core_mate)
    swap_s.start()
    zb[:, span(core * F, F), :] = summed[:, :, span(core * 128, 128)]
    swap_s.wait()

    @pl.loop(1, chips)
    def _(i):
        d = lax.rem(chip + i, chips)
        remote(zb.at[d // nz * 2 + lax.rem(d, 2)], turned.at[span(chip * 2 * F, 2 * F), :], s_send, s_recv,
               r, d * 2 + core).start()

    turned[span(chip * 2 * F, 2 * F), :] = zb[y * 2 + lax.rem(z, 2)]
    if a_count > 1:
        drain(centbuf.at[pl.ds(0, a_count - 1)], c_recv)

    for steps in far:
        pass_z(steps)

    for steps in near:
        pass_y(steps)

    drain(turned.at[pl.ds(0, (chips - 1) * 2 * F), :], s_recv)
    fresh = turned[...].astype(jnp.float32).T + centbuf[...].reshape(128, width).astype(jnp.float32)
    fresh = fresh * lax.rsqrt(jnp.sum(fresh * fresh, axis=1, keepdims=True) + EPS)
    ncs[0] = fresh.astype(jnp.bfloat16)

    up = yh * nx + lax.rem(x + 1, nx)
    down = yh * nx + lax.rem(x + nx - 1, nx)
    over = (1 - yh) * nx + x

    def cut(part, side):
        first, size = ((0, CUT), (CUT, 128 - CUT))[part]
        if side is None:
            return pl.ds(first, size)
        return pl.ds(first + side * (size // 2), size // 2)

    def push(slot, to, part, side, target):
        kind = part * 3 + (0 if side is None else 1 + side)
        rows_of = cut(part, side)
        remote(ncs.at[slot, rows_of, :], ncs.at[to, rows_of, :], g_send, g_recv.at[to, kind], target, c).start()

    def arrive(slot, part, side):
        kind = part * 3 + (0 if side is None else 1 + side)
        ref = ncs.at[slot, cut(part, side), :]
        drain(ref, g_recv.at[slot, kind])

    ring = nx == 4

    def round_x(base, part):
        push(base, base + nx - 1, part, None, up)
        if ring:
            push(base, base + 1, part, None, down)

    def relay(base, part, also):
        arrive(base + nx - 1, part, None)
        if ring:
            push(base + 3, base + 2, part, 0, up)
        if also:
            push(base + nx - 1, nx + base + nx - 1, part, None, over)
        if ring:
            arrive(base + 1, part, None)
            push(base + 1, base + 2, part, 1, down)
            if also:
                push(base + 1, nx + base + 1, part, None, over)

    push(0, nx, 0, None, over)
    round_x(0, 1)
    round_x(0, 0)
    push(0, nx, 1, None, over)
    relay(0, 1, True)
    arrive(nx, 0, None)
    round_x(nx, 0)
    relay(0, 0, False)
    if ring:
        for side in range(2):
            arrive(2, 1, side)
            push(2, nx + 2, 1, side, over)

    for steps in far:
        pass_y(steps)

    relay(nx, 0, False)

    @pl.loop(0, 2 * nz)
    def _(i):
        piece = cent_id(i // nz, lax.rem(i, nz), 1 - core)
        drain(e.at[piece], e_recv.at[piece])

    if ring:
        for side in range(2):
            arrive(2, 0, side)
    arrive(nx, 1, None)

    def score(first_slot, slots, merge):
        block = ncs[first_slot:first_slot + slots].reshape(slots * 128, width)

        @pl.loop(0, tile_rows // TILE)
        def _(t):
            here = span(t * TILE, TILE)
            scores = jnp.dot(block, e[:, :, here].reshape(width, TILE), preferred_element_type=jnp.float32)
            best = jnp.max(scores, axis=0, keepdims=True)
            for k in range(TILE // 128):
                line = pl.ds(t * (TILE // 128) + k, 1)
                piece = best[:, k * 128:(k + 1) * 128]
                top[line, :] = jnp.maximum(top[line, :], piece) if merge else piece

    score(0, nx + 1, False)

    arrive(nx + nx - 1, 1, None)
    if ring:
        arrive(nx + 1, 1, None)
        for side in range(2):
            arrive(nx + 2, 0, side)
            arrive(nx + 2, 1, side)

    score(nx + 1, nx - 1, True)

    own_half = tile_lines // 2
    swap_t = remote(top.at[span((1 - core) * own_half, own_half), :], topmate, m_send.at[3], m_recv.at[3], r, core_mate)
    swap_t.start()
    for i in range(nr):
        row = (yh if i < nx else 1 - yh) * nx + lax.rem(x + i, nx)
        pltpu.make_async_copy(ncs.at[i, span(a * j_count, j_count), :], nc_out.at[span(row * j_count, j_count), :],
                              loc.at[3]).start()
    swap_t.wait()
    tops[chip] = jnp.maximum(top[span(core * own_half, own_half), :], topmate[...])

    @pl.loop(1, chips)
    def _(i):
        d = lax.rem(chip + i, chips) * 2 + core
        remote(tops.at[chip], tops.at[chip], t_send, t_recv, r, d).start()

    drain(qchip.at[pl.ds(0, chips - 1)], n_send)
    drain(e.at[pl.ds(0, 1 + len(direct))], ez_send)
    drain(e.at[pl.ds(0, 2 + 3 * len(direct) + len(far) * 2 + len(near) * 2)], ef_send)
    if a_count > 1:
        drain(centbuf.at[pl.ds(0, a_count - 1)], c_send)
    drain(got.at[pl.ds(0, nr - 1)], p_send)
    drain(turned.at[pl.ds(0, (chips - 1) * 2 * F), :], s_send)
    drain(ncs.at[pl.ds(0, nr - 1)], g_send)

    drain(tops.at[pl.ds(0, chips - 1)], t_recv)
    for aa in range(a_count):
        best = tops[2 * aa]
        for yy in range(2):
            for k in range(2):
                best = jnp.maximum(best, tops[yy * nz + 2 * aa + k])
        first = aa * tile_lines
        here = span(first + core * own_half, own_half)
        best_out[here, :] = best * inv[here, :]
        there = best_out.at[here, :]
        remote(there, there, m_send.at[4], m_recv.at[4], r, core_mate).start()
    drain(best_out.at[pl.ds(0, half), :], m_recv.at[4])
    drain(best_out.at[pl.ds(0, half), :], m_send.at[4])
    drain(tops.at[pl.ds(0, chips - 1)], t_send)
    drain(nc_out, loc.at[3])


def per_device(nx, nz, embeddings, assigned, centroids):
    nr, nc, chips = 2 * nx, 4 * nz, 2 * nz
    rows = embeddings.shape[0]
    owned, width = centroids.shape
    a_count = nz // 2
    tile_rows = rows // a_count
    lines = rows // 128
    j_count = 256 // nz
    bf, fl = jnp.bfloat16, jnp.float32
    dma = pltpu.SemaphoreType.DMA
    vmem = pl.BlockSpec(memory_space=pltpu.VMEM)
    hbm = pl.BlockSpec(memory_space=pltpu.HBM)
    out, best = pl.pallas_call(
        functools.partial(kernel, nx, nz),
        out_shape=(jax.ShapeDtypeStruct((owned, width), bf), jax.ShapeDtypeStruct((lines, 128), fl)),
        in_specs=[hbm, vmem, hbm],
        out_specs=(hbm, vmem),
        scratch_shapes=[
            pltpu.VMEM((F, rows), bf),
            pltpu.VMEM((lines, 128), fl),
            pltpu.VMEM((lines // 2, 128), fl),
            pltpu.VMEM((chips, lines // 2, 128), bf),
            pltpu.VMEM((lines, 128), fl),
            pltpu.VMEM((lines, 128), fl),
            pltpu.VMEM((lines, 128), fl),
            pltpu.VMEM((256, rows), bf),
            pltpu.VMEM((F, rows), bf),
            pltpu.VMEM((nc, F, tile_rows), bf),
            pltpu.VMEM((2 * nr * F, 1024), bf),
            pltpu.VMEM((2 * nr * F, 256), fl),
            pltpu.VMEM((4 * nr * F, 256), bf),
            pltpu.VMEM((nr, 128, 256), bf),
            pltpu.VMEM((4, F, 256), bf),
            pltpu.VMEM((4, 2 * F, 128), bf),
            pltpu.VMEM((width, 128), bf),
            pltpu.VMEM((a_count, j_count, width), bf),
            pltpu.VMEM((nr, 128, width), bf),
            pltpu.VMEM((tile_rows // 128, 128), fl),
            pltpu.VMEM((tile_rows // 256, 128), fl),
            pltpu.VMEM((chips, tile_rows // 256, 128), fl),
            dma((4,)), dma((5,)), dma((5,)), dma, dma, dma, dma, dma((nc,)), dma, dma,
            dma, dma, dma, dma, dma, dma((nr, 6)), dma, dma,
        ],
        compiler_params=pltpu.CompilerParams(
            collective_id=0, has_side_effects=True, vmem_limit_bytes=58 * 1024 * 1024),
    )(embeddings.T, assigned.reshape(lines, 128), centroids)
    return out, best.reshape(rows)


def solution(mesh):
    nx, nz = mesh.shape["row"] // 2, mesh.shape["cent"] // 4
    return jax.shard_map(
        functools.partial(per_device, nx, nz),
        mesh=mesh,
        in_specs=(P("row", "cent"), P("row"), P("cent", None)),
        out_specs=(P("cent", None), P("row")),
        check_vma=False,
    )
```

```python
import functools

import jax
import jax.numpy as jnp
from jax import lax
from jax.experimental import pallas as pl
from jax.experimental.pallas import tpu as pltpu
from jax.sharding import PartitionSpec as P

MESH = pl.DeviceIdType.MESH
F = 32
EPS = 1e-06
CHUNK = 4096
CUT = 64
TILE = 1024


def kernel(nx, nz, x_hbm, id_ref, cent_hbm, nc_out, best_out,
           x_ref, q, qmate, qchip, inv, lanes, lows, hot, spread, e, acc, part, got, summed, zb, turned, centbuf, ncs,
           top, topmate, tops, loc, m_send, m_recv, n_send, n_recv, ez_send, ef_send, e_recv, c_send, c_recv,
           p_send, p_recv, s_send, s_recv, g_send, g_recv, t_send, t_recv):
    nr = 2 * nx
    nc = 4 * nz
    chips = 2 * nz
    rows = x_ref.shape[1]
    lines = rows // 128
    half = lines // 2
    a_count = nz // 2
    tile_rows = rows // a_count
    tile_lines = tile_rows // 128
    j_count = 256 // nz
    width = nc * F
    r = lax.axis_index("row")
    c = lax.axis_index("cent")
    core = lax.rem(c, 2)
    z = lax.rem(c // 2, nz)
    y = c // (2 * nz)
    chip = c // 2
    a = z // 2
    x = lax.rem(r, nx)
    yh = r // nx

    def cent_id(yy, zz, cc):
        return yy * (2 * nz) + zz * 2 + cc

    core_mate = cent_id(y, z, 1 - core)
    y_mate = cent_id(1 - y, z, core)

    def remote(src, dst, send, recv, row, cent):
        return pltpu.make_async_remote_copy(
            src_ref=src, dst_ref=dst, send_sem=send, recv_sem=recv,
            device_id=(row, cent), device_id_type=MESH)

    def drain(ref, sem):
        pltpu.make_async_copy(ref, ref, sem).wait()

    def span(start, size):
        return pl.ds(pl.multiple_of(start, size), size)

    in_x = pltpu.make_async_copy(x_hbm, x_ref, loc.at[0])
    in_x.start()
    own_c = pltpu.make_async_copy(cent_hbm.at[span(r * j_count, j_count), :], centbuf.at[a], loc.at[1])
    own_c.start()
    barrier = pltpu.get_barrier_semaphore()
    pl.semaphore_signal(barrier, inc=1, device_id=(r, core_mate), device_id_type=MESH)

    @pl.loop(1, chips)
    def _(i):
        d = lax.rem(chip + i, chips) * 2 + core
        pl.semaphore_signal(barrier, inc=1, device_id=(r, d), device_id_type=MESH)

    @pl.loop(1, nr)
    def _(i):
        pl.semaphore_signal(barrier, inc=1, device_id=(lax.rem(r + i, nr), c), device_id_type=MESH)

    ids = id_ref[...]
    cc = ids // (nr * j_count)
    zz = lax.rem(cc // 2, nz)
    lanes[...] = (lax.rem(cc, 2) * 128 + (zz // 2) * j_count + lax.rem(ids, j_count)).astype(jnp.float32)
    ahead = lax.rem(lax.rem(ids, nr * j_count) // j_count + (2 * nr - 1) - r, nr)
    lows[...] = (ahead * 4 + (cc // (2 * nz)) * 2 + lax.rem(zz, 2)).astype(jnp.float32)

    in_x.wait()

    @pl.loop(0, lines // 8)
    def _(t):
        wide = x_ref[:, span(t * 1024, 1024)].astype(jnp.float32)
        squares = jnp.sum(wide * wide, axis=0, keepdims=True)
        q[span(t * 8, 8), :] = jnp.concatenate([squares[:, k * 128:(k + 1) * 128] for k in range(8)], axis=0)

    pl.semaphore_wait(barrier, 1 + chips - 1 + nr - 1)

    swap_q = remote(q.at[span((1 - core) * half, half), :], qmate, m_send.at[0], m_recv.at[0], r, core_mate)
    swap_q.start()
    own_e = pltpu.make_async_copy(x_ref.at[:, span(a * tile_rows, tile_rows)], e.at[c], loc.at[2])
    own_e.start()
    swap_q.wait()
    qchip[chip] = (q[span(core * half, half), :] + qmate[...]).astype(jnp.bfloat16)

    @pl.loop(1, chips)
    def _(i):
        d = lax.rem(chip + i, chips) * 2 + core
        remote(qchip.at[chip], qchip.at[chip], n_send, n_recv, r, d).start()

    outward = 2 * lax.rem(z, 2) - 1

    def at_z(steps):
        return lax.rem(z + outward * steps + nz, nz)

    z_mate = cent_id(y, at_z(-1), core)
    direct = (1, 2, 3) if nz == 8 else ()
    for steps in (-1, 1, -2, 3) if nz == 8 else (-1,):
        to = at_z(steps)
        remote(x_ref.at[:, span((to // 2) * tile_rows, tile_rows)], e.at[c], ez_send, e_recv.at[c],
               r, cent_id(y, to, core)).start()

    own_c.wait()

    @pl.loop(1, a_count)
    def _(i):
        remote(centbuf.at[a], centbuf.at[a], c_send, c_recv, r, cent_id(y, lax.rem(z + 2 * i, nz), core)).start()

    def pass_on(piece, to_z, to_y):
        if to_z:
            remote(e.at[piece], e.at[piece], ef_send, e_recv.at[piece], r, z_mate).start()
        if to_y:
            remote(e.at[piece], e.at[piece], ef_send, e_recv.at[piece], r, y_mate).start()
        remote(e.at[piece], e.at[piece], ef_send, e_recv.at[piece], r, core_mate).start()

    def pass_z(steps):
        piece = cent_id(y, at_z(steps), core)
        drain(e.at[piece], e_recv.at[piece])
        pass_on(piece, steps > 0, steps > 0)

    def pass_y(steps):
        piece = cent_id(1 - y, at_z(steps), core)
        drain(e.at[piece], e_recv.at[piece])
        pass_on(piece, steps >= 0, False)

    near, far = ((0, 1, 2, 3), (-1, -2, -3, -4)) if nz == 8 else ((0,), (-1,))

    own_e.wait()
    pass_on(c, False, True)

    def along(block):
        return jnp.concatenate([block[k:k + 1, :] for k in range(8)], axis=1)

    def packed(block):
        return jnp.broadcast_to(along(block), (16, 1024)).astype(jnp.bfloat16)

    @pl.loop(0, lines // 8)
    def _(t):
        here, lines8 = span(t * 1024, 1024), span(t * 8, 8)
        lane_b, low_b = packed(lanes[lines8, :]), packed(lows[lines8, :])
        iota = lax.broadcasted_iota(jnp.int32, (16, 1024), 0).astype(jnp.float32)
        for k in range(16):
            hot[k * 16:(k + 1) * 16, here] = jnp.where(
                lane_b == (iota + k * 16).astype(jnp.bfloat16), jnp.bfloat16(1), jnp.bfloat16(0))
        for k in range(F // 16):
            mine = x_ref[k * 16:(k + 1) * 16, here]
            for j in range(4 * nr):
                at = j * F + k * 16
                spread[at:at + 16, here] = jnp.where(low_b == jnp.bfloat16(j), mine, jnp.bfloat16(0))

    drain(qchip.at[pl.ds(0, chips - 1)], n_recv)
    squares = qchip[0].astype(jnp.float32)
    for i in range(1, chips):
        squares = squares + qchip[i].astype(jnp.float32)
    own_inv = inv.at[span(core * half, half), :]
    own_inv[...] = lax.rsqrt(squares + EPS)
    swap_i = remote(own_inv, own_inv, m_send.at[1], m_recv.at[1], r, core_mate)
    swap_i.start()
    swap_i.wait()

    group = nr // 2
    block_rows = 4 * F

    @pl.loop(0, lines // 8)
    def _(t):
        here = span(t * 1024, 1024)
        scale = packed(inv[span(t * 8, 8), :])
        for k in range(16):
            hot[k * 16:(k + 1) * 16, here] = hot[k * 16:(k + 1) * 16, here] * scale

    for g in range(2):
        @pl.loop(0, rows // CHUNK)
        def _(t):
            here = span(t * CHUNK, CHUNK)
            product = lax.dot_general(
                spread[g * group * block_rows:(g + 1) * group * block_rows, here], hot[:, here],
                (((1,), (1,)), ((), ())), preferred_element_type=jnp.float32)

            @pl.when(t == 0)
            def _():
                acc[...] = product

            @pl.when(t > 0)
            def _():
                acc[...] += product

        part[g * group * block_rows:(g + 1) * group * block_rows, :] = acc[...].astype(jnp.bfloat16)
        for k in range(g * group, (g + 1) * group):
            if k < nr - 1:
                remote(part.at[pl.ds(k * block_rows, block_rows), :], got.at[r], p_send, p_recv,
                       lax.rem(r + 1 + k, nr), c).start()

    got[r] = part[(nr - 1) * block_rows:, :]

    for steps in near[1:]:
        pass_z(steps)

    drain(got.at[pl.ds(0, nr - 1)], p_recv)
    total = got[0].astype(jnp.float32)
    for i in range(1, nr):
        total = total + got[i].astype(jnp.float32)
    summed[...] = total.astype(jnp.bfloat16).reshape(4, F, 256)

    swap_s = remote(summed.at[:, :, span((1 - core) * 128, 128)], zb.at[:, span(core * F, F), :],
                    m_send.at[2], m_recv.at[2], r, core_mate)
    swap_s.start()
    zb[:, span(core * F, F), :] = summed[:, :, span(core * 128, 128)]
    swap_s.wait()

    @pl.loop(1, chips)
    def _(i):
        d = lax.rem(chip + i, chips)
        remote(zb.at[d // nz * 2 + lax.rem(d, 2)], turned.at[span(chip * 2 * F, 2 * F), :], s_send, s_recv,
               r, d * 2 + core).start()

    turned[span(chip * 2 * F, 2 * F), :] = zb[y * 2 + lax.rem(z, 2)]
    if a_count > 1:
        drain(centbuf.at[pl.ds(0, a_count - 1)], c_recv)

    for steps in far:
        pass_z(steps)

    for steps in near:
        pass_y(steps)

    drain(turned.at[pl.ds(0, (chips - 1) * 2 * F), :], s_recv)
    fresh = turned[...].astype(jnp.float32).T + centbuf[...].reshape(128, width).astype(jnp.float32)
    fresh = fresh * lax.rsqrt(jnp.sum(fresh * fresh, axis=1, keepdims=True) + EPS)
    ncs[0] = fresh.astype(jnp.bfloat16)

    up = yh * nx + lax.rem(x + 1, nx)
    down = yh * nx + lax.rem(x + nx - 1, nx)
    over = (1 - yh) * nx + x

    def cut(part, side):
        first, size = ((0, CUT), (CUT, 128 - CUT))[part]
        if side is None:
            return pl.ds(first, size)
        return pl.ds(first + side * (size // 2), size // 2)

    def push(slot, to, part, side, target):
        kind = part * 3 + (0 if side is None else 1 + side)
        rows_of = cut(part, side)
        remote(ncs.at[slot, rows_of, :], ncs.at[to, rows_of, :], g_send, g_recv.at[to, kind], target, c).start()

    def arrive(slot, part, side):
        kind = part * 3 + (0 if side is None else 1 + side)
        ref = ncs.at[slot, cut(part, side), :]
        drain(ref, g_recv.at[slot, kind])

    ring = nx == 4

    def round_x(base, part):
        push(base, base + nx - 1, part, None, up)
        if ring:
            push(base, base + 1, part, None, down)

    def relay(base, part, also):
        arrive(base + nx - 1, part, None)
        if ring:
            push(base + 3, base + 2, part, 0, up)
        if also:
            push(base + nx - 1, nx + base + nx - 1, part, None, over)
        if ring:
            arrive(base + 1, part, None)
            push(base + 1, base + 2, part, 1, down)
            if also:
                push(base + 1, nx + base + 1, part, None, over)

    push(0, nx, 0, None, over)
    round_x(0, 1)
    round_x(0, 0)
    push(0, nx, 1, None, over)
    relay(0, 1, True)
    arrive(nx, 0, None)
    round_x(nx, 0)
    relay(0, 0, False)
    if ring:
        for side in range(2):
            arrive(2, 1, side)
            push(2, nx + 2, 1, side, over)

    for steps in far:
        pass_y(steps)

    relay(nx, 0, False)

    @pl.loop(0, 2 * nz)
    def _(i):
        piece = cent_id(i // nz, lax.rem(i, nz), 1 - core)
        drain(e.at[piece], e_recv.at[piece])

    if ring:
        for side in range(2):
            arrive(2, 0, side)
    arrive(nx, 1, None)

    def score(first_slot, slots, merge):
        block = ncs[first_slot:first_slot + slots].reshape(slots * 128, width)

        @pl.loop(0, tile_rows // TILE)
        def _(t):
            here = span(t * TILE, TILE)
            scores = jnp.dot(block, e[:, :, here].reshape(width, TILE), preferred_element_type=jnp.float32)
            best = jnp.max(scores, axis=0, keepdims=True)
            for k in range(TILE // 128):
                line = pl.ds(t * (TILE // 128) + k, 1)
                piece = best[:, k * 128:(k + 1) * 128]
                top[line, :] = jnp.maximum(top[line, :], piece) if merge else piece

    score(0, nx + 1, False)

    arrive(nx + nx - 1, 1, None)
    if ring:
        arrive(nx + 1, 1, None)
        for side in range(2):
            arrive(nx + 2, 0, side)
            arrive(nx + 2, 1, side)

    score(nx + 1, nx - 1, True)

    own_half = tile_lines // 2
    swap_t = remote(top.at[span((1 - core) * own_half, own_half), :], topmate, m_send.at[3], m_recv.at[3], r, core_mate)
    swap_t.start()
    for i in range(nr):
        row = (yh if i < nx else 1 - yh) * nx + lax.rem(x + i, nx)
        pltpu.make_async_copy(ncs.at[i, span(a * j_count, j_count), :], nc_out.at[span(row * j_count, j_count), :],
                              loc.at[3]).start()
    swap_t.wait()
    tops[chip] = jnp.maximum(top[span(core * own_half, own_half), :], topmate[...])

    @pl.loop(1, chips)
    def _(i):
        d = lax.rem(chip + i, chips) * 2 + core
        remote(tops.at[chip], tops.at[chip], t_send, t_recv, r, d).start()

    drain(qchip.at[pl.ds(0, chips - 1)], n_send)
    drain(e.at[pl.ds(0, 1 + len(direct))], ez_send)
    drain(e.at[pl.ds(0, 2 + 3 * len(direct) + len(far) * 2 + len(near) * 2)], ef_send)
    if a_count > 1:
        drain(centbuf.at[pl.ds(0, a_count - 1)], c_send)
    drain(got.at[pl.ds(0, nr - 1)], p_send)
    drain(turned.at[pl.ds(0, (chips - 1) * 2 * F), :], s_send)
    drain(ncs.at[pl.ds(0, nr - 1)], g_send)

    drain(tops.at[pl.ds(0, chips - 1)], t_recv)
    for aa in range(a_count):
        best = tops[2 * aa]
        for yy in range(2):
            for k in range(2):
                best = jnp.maximum(best, tops[yy * nz + 2 * aa + k])
        first = aa * tile_lines
        here = span(first + core * own_half, own_half)
        best_out[here, :] = best * inv[here, :]
        there = best_out.at[here, :]
        remote(there, there, m_send.at[4], m_recv.at[4], r, core_mate).start()
    drain(best_out.at[pl.ds(0, half), :], m_recv.at[4])
    drain(best_out.at[pl.ds(0, half), :], m_send.at[4])
    drain(tops.at[pl.ds(0, chips - 1)], t_send)
    drain(nc_out, loc.at[3])


def per_device(nx, nz, embeddings, assigned, centroids):
    nr, nc, chips = 2 * nx, 4 * nz, 2 * nz
    rows = embeddings.shape[0]
    owned, width = centroids.shape
    a_count = nz // 2
    tile_rows = rows // a_count
    lines = rows // 128
    j_count = 256 // nz
    bf, fl = jnp.bfloat16, jnp.float32
    dma = pltpu.SemaphoreType.DMA
    vmem = pl.BlockSpec(memory_space=pltpu.VMEM)
    hbm = pl.BlockSpec(memory_space=pltpu.HBM)
    out, best = pl.pallas_call(
        functools.partial(kernel, nx, nz),
        out_shape=(jax.ShapeDtypeStruct((owned, width), bf), jax.ShapeDtypeStruct((lines, 128), fl)),
        in_specs=[hbm, vmem, hbm],
        out_specs=(hbm, vmem),
        scratch_shapes=[
            pltpu.VMEM((F, rows), bf),
            pltpu.VMEM((lines, 128), fl),
            pltpu.VMEM((lines // 2, 128), fl),
            pltpu.VMEM((chips, lines // 2, 128), bf),
            pltpu.VMEM((lines, 128), fl),
            pltpu.VMEM((lines, 128), fl),
            pltpu.VMEM((lines, 128), fl),
            pltpu.VMEM((256, rows), bf),
            pltpu.VMEM((4 * nr * F, rows), bf),
            pltpu.VMEM((nc, F, tile_rows), bf),
            pltpu.VMEM((2 * nr * F, 256), fl),
            pltpu.VMEM((4 * nr * F, 256), bf),
            pltpu.VMEM((nr, 128, 256), bf),
            pltpu.VMEM((4, F, 256), bf),
            pltpu.VMEM((4, 2 * F, 128), bf),
            pltpu.VMEM((width, 128), bf),
            pltpu.VMEM((a_count, j_count, width), bf),
            pltpu.VMEM((nr, 128, width), bf),
            pltpu.VMEM((tile_rows // 128, 128), fl),
            pltpu.VMEM((tile_rows // 256, 128), fl),
            pltpu.VMEM((chips, tile_rows // 256, 128), fl),
            dma((4,)), dma((5,)), dma((5,)), dma, dma, dma, dma, dma((nc,)), dma, dma,
            dma, dma, dma, dma, dma, dma((nr, 6)), dma, dma,
        ],
        compiler_params=pltpu.CompilerParams(
            collective_id=0, has_side_effects=True, vmem_limit_bytes=58 * 1024 * 1024),
    )(embeddings.T, assigned.reshape(lines, 128), centroids)
    return out, best.reshape(rows)


def solution(mesh):
    nx, nz = mesh.shape["row"] // 2, mesh.shape["cent"] // 4
    return jax.shard_map(
        functools.partial(per_device, nx, nz),
        mesh=mesh,
        in_specs=(P("row", "cent"), P("row"), P("cent", None)),
        out_specs=(P("cent", None), P("row")),
        check_vma=False,
    )
```

```python
import functools

import jax
import jax.numpy as jnp
from jax import lax
from jax.experimental import pallas as pl
from jax.experimental.pallas import tpu as pltpu
from jax.sharding import PartitionSpec as P

MESH = pl.DeviceIdType.MESH
F = 32
EPS = 1e-06
CHUNK = 4096
CUT = 64
TILE = 2048


def kernel(nx, nz, x_hbm, id_ref, cent_hbm, nc_out, best_out,
           x_ref, q, qmate, qchip, inv, lanes, lows, hot, spread, e, acc, part, got, summed, zb, turned, centbuf, ncs,
           top, topmate, tops, loc, m_send, m_recv, n_send, n_recv, ez_send, ef_send, e_recv, c_send, c_recv,
           p_send, p_recv, s_send, s_recv, g_send, g_recv, t_send, t_recv):
    nr = 2 * nx
    nc = 4 * nz
    chips = 2 * nz
    rows = x_ref.shape[1]
    lines = rows // 128
    half = lines // 2
    a_count = nz // 2
    tile_rows = rows // a_count
    tile_lines = tile_rows // 128
    j_count = 256 // nz
    width = nc * F
    r = lax.axis_index("row")
    c = lax.axis_index("cent")
    core = lax.rem(c, 2)
    z = lax.rem(c // 2, nz)
    y = c // (2 * nz)
    chip = c // 2
    a = z // 2
    x = lax.rem(r, nx)
    yh = r // nx

    def cent_id(yy, zz, cc):
        return yy * (2 * nz) + zz * 2 + cc

    core_mate = cent_id(y, z, 1 - core)
    y_mate = cent_id(1 - y, z, core)

    def remote(src, dst, send, recv, row, cent):
        return pltpu.make_async_remote_copy(
            src_ref=src, dst_ref=dst, send_sem=send, recv_sem=recv,
            device_id=(row, cent), device_id_type=MESH)

    def drain(ref, sem):
        pltpu.make_async_copy(ref, ref, sem).wait()

    def span(start, size):
        return pl.ds(pl.multiple_of(start, size), size)

    in_x = pltpu.make_async_copy(x_hbm, x_ref, loc.at[0])
    in_x.start()
    own_c = pltpu.make_async_copy(cent_hbm.at[span(r * j_count, j_count), :], centbuf.at[a], loc.at[1])
    own_c.start()
    barrier = pltpu.get_barrier_semaphore()
    pl.semaphore_signal(barrier, inc=1, device_id=(r, core_mate), device_id_type=MESH)

    @pl.loop(1, chips)
    def _(i):
        d = lax.rem(chip + i, chips) * 2 + core
        pl.semaphore_signal(barrier, inc=1, device_id=(r, d), device_id_type=MESH)

    @pl.loop(1, nr)
    def _(i):
        pl.semaphore_signal(barrier, inc=1, device_id=(lax.rem(r + i, nr), c), device_id_type=MESH)

    ids = id_ref[...]
    cc = ids // (nr * j_count)
    zz = lax.rem(cc // 2, nz)
    lanes[...] = (lax.rem(cc, 2) * 128 + (zz // 2) * j_count + lax.rem(ids, j_count)).astype(jnp.float32)
    ahead = lax.rem(lax.rem(ids, nr * j_count) // j_count + (2 * nr - 1) - r, nr)
    lows[...] = (ahead * 4 + (cc // (2 * nz)) * 2 + lax.rem(zz, 2)).astype(jnp.float32)

    in_x.wait()

    @pl.loop(0, lines // 8)
    def _(t):
        wide = x_ref[:, span(t * 1024, 1024)].astype(jnp.float32)
        squares = jnp.sum(wide * wide, axis=0, keepdims=True)
        q[span(t * 8, 8), :] = jnp.concatenate([squares[:, k * 128:(k + 1) * 128] for k in range(8)], axis=0)

    pl.semaphore_wait(barrier, 1 + chips - 1 + nr - 1)

    swap_q = remote(q.at[span((1 - core) * half, half), :], qmate, m_send.at[0], m_recv.at[0], r, core_mate)
    swap_q.start()
    own_e = pltpu.make_async_copy(x_ref.at[:, span(a * tile_rows, tile_rows)], e.at[c], loc.at[2])
    own_e.start()
    swap_q.wait()
    qchip[chip] = (q[span(core * half, half), :] + qmate[...]).astype(jnp.bfloat16)

    @pl.loop(1, chips)
    def _(i):
        d = lax.rem(chip + i, chips) * 2 + core
        remote(qchip.at[chip], qchip.at[chip], n_send, n_recv, r, d).start()

    outward = 2 * lax.rem(z, 2) - 1

    def at_z(steps):
        return lax.rem(z + outward * steps + nz, nz)

    z_mate = cent_id(y, at_z(-1), core)
    direct = (1, 2, 3) if nz == 8 else ()
    for steps in (-1, 1, -2, 3) if nz == 8 else (-1,):
        to = at_z(steps)
        remote(x_ref.at[:, span((to // 2) * tile_rows, tile_rows)], e.at[c], ez_send, e_recv.at[c],
               r, cent_id(y, to, core)).start()

    own_c.wait()

    @pl.loop(1, a_count)
    def _(i):
        remote(centbuf.at[a], centbuf.at[a], c_send, c_recv, r, cent_id(y, lax.rem(z + 2 * i, nz), core)).start()

    def pass_on(piece, to_z, to_y):
        if to_z:
            remote(e.at[piece], e.at[piece], ef_send, e_recv.at[piece], r, z_mate).start()
        if to_y:
            remote(e.at[piece], e.at[piece], ef_send, e_recv.at[piece], r, y_mate).start()
        remote(e.at[piece], e.at[piece], ef_send, e_recv.at[piece], r, core_mate).start()

    def pass_z(steps):
        piece = cent_id(y, at_z(steps), core)
        drain(e.at[piece], e_recv.at[piece])
        pass_on(piece, steps > 0, steps > 0 or steps in (-1, -2))

    def pass_y(steps):
        piece = cent_id(1 - y, at_z(steps), core)
        drain(e.at[piece], e_recv.at[piece])
        pass_on(piece, steps in (2, 3), False)

    near, far = ((0, 1, 2, 3), (-1, -2, -3, -4)) if nz == 8 else ((0,), (-1,))

    own_e.wait()
    pass_on(c, False, True)

    def along(block):
        return jnp.concatenate([block[k:k + 1, :] for k in range(8)], axis=1)

    def packed(block):
        return jnp.broadcast_to(along(block), (16, 1024)).astype(jnp.bfloat16)

    @pl.loop(0, lines // 8)
    def _(t):
        here, lines8 = span(t * 1024, 1024), span(t * 8, 8)
        lane_b, low_b = packed(lanes[lines8, :]), packed(lows[lines8, :])
        iota = lax.broadcasted_iota(jnp.int32, (16, 1024), 0).astype(jnp.float32)
        for k in range(16):
            hot[k * 16:(k + 1) * 16, here] = jnp.where(
                lane_b == (iota + k * 16).astype(jnp.bfloat16), jnp.bfloat16(1), jnp.bfloat16(0))
        for k in range(F // 16):
            mine = x_ref[k * 16:(k + 1) * 16, here]
            for j in range(4 * nr):
                at = j * F + k * 16
                spread[at:at + 16, here] = jnp.where(low_b == jnp.bfloat16(j), mine, jnp.bfloat16(0))

    drain(qchip.at[pl.ds(0, chips - 1)], n_recv)
    squares = qchip[0].astype(jnp.float32)
    for i in range(1, chips):
        squares = squares + qchip[i].astype(jnp.float32)
    own_inv = inv.at[span(core * half, half), :]
    own_inv[...] = lax.rsqrt(squares + EPS)
    swap_i = remote(own_inv, own_inv, m_send.at[1], m_recv.at[1], r, core_mate)
    swap_i.start()
    swap_i.wait()

    group = nr // 2
    block_rows = 4 * F

    @pl.loop(0, lines // 8)
    def _(t):
        here = span(t * 1024, 1024)
        scale = packed(inv[span(t * 8, 8), :])
        for k in range(16):
            hot[k * 16:(k + 1) * 16, here] = hot[k * 16:(k + 1) * 16, here] * scale

    for g in range(2):
        @pl.loop(0, rows // CHUNK)
        def _(t):
            here = span(t * CHUNK, CHUNK)
            product = lax.dot_general(
                spread[g * group * block_rows:(g + 1) * group * block_rows, here], hot[:, here],
                (((1,), (1,)), ((), ())), preferred_element_type=jnp.float32)

            @pl.when(t == 0)
            def _():
                acc[...] = product

            @pl.when(t > 0)
            def _():
                acc[...] += product

        part[g * group * block_rows:(g + 1) * group * block_rows, :] = acc[...].astype(jnp.bfloat16)
        for k in range(g * group, (g + 1) * group):
            if k < nr - 1:
                remote(part.at[pl.ds(k * block_rows, block_rows), :], got.at[r], p_send, p_recv,
                       lax.rem(r + 1 + k, nr), c).start()

    got[r] = part[(nr - 1) * block_rows:, :]

    pass_z(-1)
    for steps in near[1:]:
        pass_z(steps)

    drain(got.at[pl.ds(0, nr - 1)], p_recv)
    total = got[0].astype(jnp.float32)
    for i in range(1, nr):
        total = total + got[i].astype(jnp.float32)
    summed[...] = total.astype(jnp.bfloat16).reshape(4, F, 256)

    swap_s = remote(summed.at[:, :, span((1 - core) * 128, 128)], zb.at[:, span(core * F, F), :],
                    m_send.at[2], m_recv.at[2], r, core_mate)
    swap_s.start()
    zb[:, span(core * F, F), :] = summed[:, :, span(core * 128, 128)]
    swap_s.wait()

    @pl.loop(1, chips)
    def _(i):
        d = lax.rem(chip + i, chips)
        remote(zb.at[d // nz * 2 + lax.rem(d, 2)], turned.at[span(chip * 2 * F, 2 * F), :], s_send, s_recv,
               r, d * 2 + core).start()

    turned[span(chip * 2 * F, 2 * F), :] = zb[y * 2 + lax.rem(z, 2)]
    if a_count > 1:
        drain(centbuf.at[pl.ds(0, a_count - 1)], c_recv)

    for steps in far[1:]:
        pass_z(steps)

    for steps in near:
        pass_y(steps)

    drain(turned.at[pl.ds(0, (chips - 1) * 2 * F), :], s_recv)
    fresh = turned[...].astype(jnp.float32).T + centbuf[...].reshape(128, width).astype(jnp.float32)
    fresh = fresh * lax.rsqrt(jnp.sum(fresh * fresh, axis=1, keepdims=True) + EPS)
    ncs[0] = fresh.astype(jnp.bfloat16)

    up = yh * nx + lax.rem(x + 1, nx)
    down = yh * nx + lax.rem(x + nx - 1, nx)
    over = (1 - yh) * nx + x

    def cut(part, side):
        first, size = ((0, CUT), (CUT, 128 - CUT))[part]
        if side is None:
            return pl.ds(first, size)
        return pl.ds(first + side * (size // 2), size // 2)

    def push(slot, to, part, side, target):
        kind = part * 3 + (0 if side is None else 1 + side)
        rows_of = cut(part, side)
        remote(ncs.at[slot, rows_of, :], ncs.at[to, rows_of, :], g_send, g_recv.at[to, kind], target, c).start()

    def arrive(slot, part, side):
        kind = part * 3 + (0 if side is None else 1 + side)
        ref = ncs.at[slot, cut(part, side), :]
        drain(ref, g_recv.at[slot, kind])

    ring = nx == 4

    def round_x(base, part):
        push(base, base + nx - 1, part, None, up)
        if ring:
            push(base, base + 1, part, None, down)

    def relay(base, part, also):
        arrive(base + nx - 1, part, None)
        if ring:
            push(base + 3, base + 2, part, 0, up)
        if also:
            push(base + nx - 1, nx + base + nx - 1, part, None, over)
        if ring:
            arrive(base + 1, part, None)
            push(base + 1, base + 2, part, 1, down)
            if also:
                push(base + 1, nx + base + 1, part, None, over)

    round_x(0, 1)
    push(0, nx, 0, None, over)
    round_x(0, 0)
    push(0, nx, 1, None, over)
    relay(0, 1, True)
    arrive(nx, 0, None)
    round_x(nx, 0)
    relay(0, 0, False)
    if ring:
        for side in range(2):
            arrive(2, 1, side)
            push(2, nx + 2, 1, side, over)

    for steps in far:
        pass_y(steps)

    relay(nx, 0, False)

    @pl.loop(0, 2 * nz)
    def _(i):
        piece = cent_id(i // nz, lax.rem(i, nz), 1 - core)
        drain(e.at[piece], e_recv.at[piece])

    if ring:
        for side in range(2):
            arrive(2, 0, side)
    arrive(nx, 1, None)

    def score(first_slot, slots, merge):
        block = ncs[first_slot:first_slot + slots].reshape(slots * 128, width)

        @pl.loop(0, tile_rows // TILE)
        def _(t):
            here = span(t * TILE, TILE)
            scores = jnp.dot(block, e[:, :, here].reshape(width, TILE), preferred_element_type=jnp.float32)
            best = jnp.max(scores, axis=0, keepdims=True)
            for k in range(TILE // 128):
                line = pl.ds(t * (TILE // 128) + k, 1)
                piece = best[:, k * 128:(k + 1) * 128]
                top[line, :] = jnp.maximum(top[line, :], piece) if merge else piece

    score(0, nx + 1, False)

    arrive(nx + nx - 1, 1, None)
    if ring:
        arrive(nx + 1, 1, None)
        for side in range(2):
            arrive(nx + 2, 0, side)
            arrive(nx + 2, 1, side)

    score(nx + 1, nx - 1, True)

    own_half = tile_lines // 2
    swap_t = remote(top.at[span((1 - core) * own_half, own_half), :], topmate, m_send.at[3], m_recv.at[3], r, core_mate)
    swap_t.start()
    for i in range(nr):
        row = (yh if i < nx else 1 - yh) * nx + lax.rem(x + i, nx)
        pltpu.make_async_copy(ncs.at[i, span(a * j_count, j_count), :], nc_out.at[span(row * j_count, j_count), :],
                              loc.at[3]).start()
    swap_t.wait()
    tops[chip] = jnp.maximum(top[span(core * own_half, own_half), :], topmate[...])

    @pl.loop(1, chips)
    def _(i):
        d = lax.rem(chip + i, chips) * 2 + core
        remote(tops.at[chip], tops.at[chip], t_send, t_recv, r, d).start()

    drain(qchip.at[pl.ds(0, chips - 1)], n_send)
    drain(e.at[pl.ds(0, 1 + len(direct))], ez_send)
    drain(e.at[pl.ds(0, 2 + 3 * len(direct) + len(far) * 2 + len(near) * 2)], ef_send)
    if a_count > 1:
        drain(centbuf.at[pl.ds(0, a_count - 1)], c_send)
    drain(got.at[pl.ds(0, nr - 1)], p_send)
    drain(turned.at[pl.ds(0, (chips - 1) * 2 * F), :], s_send)
    drain(ncs.at[pl.ds(0, nr - 1)], g_send)

    drain(tops.at[pl.ds(0, chips - 1)], t_recv)
    for aa in range(a_count):
        best = tops[2 * aa]
        for yy in range(2):
            for k in range(2):
                best = jnp.maximum(best, tops[yy * nz + 2 * aa + k])
        first = aa * tile_lines
        here = span(first + core * own_half, own_half)
        best_out[here, :] = best * inv[here, :]
        there = best_out.at[here, :]
        remote(there, there, m_send.at[4], m_recv.at[4], r, core_mate).start()
    drain(best_out.at[pl.ds(0, half), :], m_recv.at[4])
    drain(best_out.at[pl.ds(0, half), :], m_send.at[4])
    drain(tops.at[pl.ds(0, chips - 1)], t_send)
    drain(nc_out, loc.at[3])


def per_device(nx, nz, embeddings, assigned, centroids):
    nr, nc, chips = 2 * nx, 4 * nz, 2 * nz
    rows = embeddings.shape[0]
    owned, width = centroids.shape
    a_count = nz // 2
    tile_rows = rows // a_count
    lines = rows // 128
    j_count = 256 // nz
    bf, fl = jnp.bfloat16, jnp.float32
    dma = pltpu.SemaphoreType.DMA
    vmem = pl.BlockSpec(memory_space=pltpu.VMEM)
    hbm = pl.BlockSpec(memory_space=pltpu.HBM)
    out, best = pl.pallas_call(
        functools.partial(kernel, nx, nz),
        out_shape=(jax.ShapeDtypeStruct((owned, width), bf), jax.ShapeDtypeStruct((lines, 128), fl)),
        in_specs=[hbm, vmem, hbm],
        out_specs=(hbm, vmem),
        scratch_shapes=[
            pltpu.VMEM((F, rows), bf),
            pltpu.VMEM((lines, 128), fl),
            pltpu.VMEM((lines // 2, 128), fl),
            pltpu.VMEM((chips, lines // 2, 128), bf),
            pltpu.VMEM((lines, 128), fl),
            pltpu.VMEM((lines, 128), fl),
            pltpu.VMEM((lines, 128), fl),
            pltpu.VMEM((256, rows), bf),
            pltpu.VMEM((4 * nr * F, rows), bf),
            pltpu.VMEM((nc, F, tile_rows), bf),
            pltpu.VMEM((2 * nr * F, 256), fl),
            pltpu.VMEM((4 * nr * F, 256), bf),
            pltpu.VMEM((nr, 128, 256), bf),
            pltpu.VMEM((4, F, 256), bf),
            pltpu.VMEM((4, 2 * F, 128), bf),
            pltpu.VMEM((width, 128), bf),
            pltpu.VMEM((a_count, j_count, width), bf),
            pltpu.VMEM((nr, 128, width), bf),
            pltpu.VMEM((tile_rows // 128, 128), fl),
            pltpu.VMEM((tile_rows // 256, 128), fl),
            pltpu.VMEM((chips, tile_rows // 256, 128), fl),
            dma((4,)), dma((5,)), dma((5,)), dma, dma, dma, dma, dma((nc,)), dma, dma,
            dma, dma, dma, dma, dma, dma((nr, 6)), dma, dma,
        ],
        compiler_params=pltpu.CompilerParams(
            collective_id=0, has_side_effects=True, vmem_limit_bytes=58 * 1024 * 1024),
    )(embeddings.T, assigned.reshape(lines, 128), centroids)
    return out, best.reshape(rows)


def solution(mesh):
    nx, nz = mesh.shape["row"] // 2, mesh.shape["cent"] // 4
    return jax.shard_map(
        functools.partial(per_device, nx, nz),
        mesh=mesh,
        in_specs=(P("row", "cent"), P("row"), P("cent", None)),
        out_specs=(P("cent", None), P("row")),
        check_vma=False,
    )
```
